32 devices in a mesh: row: 2 (over x), col: 8 (over z, core), pole: 2 (over y).
Axes of the slice: x: 2, y: 2, z: 4, core: 2. Of those that a mesh axis runs over, the one named last changes fastest.
Arguments:
- inv_block: bfloat16 [2, 16384, 16384], P('pole', 'row', 'col'), may hold values from -6 to 6
- block_masks: int32 [2, 128, 128], P(None, 'row', 'col'), may hold values 0 or 1
- panel_first: bfloat16 [2, 16384, 512], P('pole', 'row'), may hold values from -0.046875 to 0.046875
- panel_second: bfloat16 [2, 16384, 512], P('pole', 'row'), may hold values from -0.046875 to 0.046875
- diag_inverse: bfloat16 [2, 2, 512, 512], P(None, 'pole'), may hold values from -6 to 6
- weights: float32 [2], P('pole'), may hold values from 0.3 to 1.2
Outputs:
- density_panels: bfloat16 [2, 16384, 512], P(None, ('row', 'col', 'pole'))
- density_diag: float32 [2, 512, 512], replicated
The draws below stay inside these ranges and needn't reach their ends.
All inputs are finite; a program needn't handle non-finite values. No bound on the sum of `block_masks` on one device may be relied on, other than what follows from the above.
Results may differ from the reference program's by a relative error of at most 0.0043.
Values may be sent and summed in bfloat16 or wider, within the bound.
No kernel may reach another device: no remote copies, remote signals or barrier semaphores. Data moves between devices by JAX's collectives and lax.ppermute only.
A program may use at most 192 MiB of HBM per device.

```python
import jax
import jax.numpy as jnp
from jax import lax

ORDER = 16384
WIDTH = 512
BLOCK = 128
NBLK = 128
POLES = 2


def touch_ends(array, rng, low, top_value):
    dims = array.shape
    place = [jax.random.randint(jax.random.fold_in(rng, axis), (), 0, dims[axis]) for axis in range(len(dims))]
    array = array.at[tuple(place)].set(low)
    longest = dims.index(max(dims))
    place[longest] = (place[longest] + 1) % dims[longest]
    return array.at[tuple(place)].set(top_value)


def shard_levels(stream_key, extent, split, least, top_value):
    def one(position, shards_of):
        steps = jax.random.uniform(jax.random.fold_in(jax.random.fold_in(stream_key, 6), position), (shards_of,), jnp.float32, least / len(split), top_value / len(split))
        return jnp.repeat(jnp.exp(steps), extent[position] // shards_of).reshape((-1,) + (1,) * (len(extent) - position - 1))

    level = one(*split[0])
    for cut in split[1:]:
        level = level * one(*cut)
    return level


def scatter_about(rng, shape, scale, bound, shards=(), kind=jnp.bfloat16):
    array = jax.random.normal(rng, shape, jnp.float32) * scale
    if len(shards) > 0:
        array = shard_levels(rng, shape, shards, -0.22, 0.18) * array
    return jnp.clip(array, min=-bound, max=bound).astype(kind)


def setup_inputs(seed: int = 0) -> dict:
    key_of = jax.random.split(jax.random.key(seed), 7)
    return {
        "inv_block": scatter_about(key_of[0], (POLES, ORDER, ORDER), 1.0, 6.0, ((0, 2), (1, 2), (2, 8))),
        "block_masks": touch_ends((jax.random.randint(key_of[1], (2, NBLK, NBLK), 0, 5) < 3).astype(jnp.int32), jax.random.fold_in(key_of[1], 1), 0, 1),
        "panel_first": scatter_about(key_of[2], (POLES, ORDER, WIDTH), ORDER ** -0.5, 0.046875, ((0, 2), (1, 2))),
        "panel_second": scatter_about(key_of[3], (POLES, ORDER, WIDTH), ORDER ** -0.5, 0.046875, ((0, 2), (1, 2))),
        "diag_inverse": scatter_about(key_of[4], (2, POLES, WIDTH, WIDTH), 1.0, 6.0, ((1, 2),)),
        "weights": jnp.clip(0.3 + 0.90000004 * jax.random.uniform(key_of[5], (POLES,), jnp.float32) ** shard_levels(key_of[5], (POLES,), ((0, 2),), -0.2, 0.2), 0.3, 1.2),
    }


def supernode(inv_block, mask_rows, factor, diag_inv, weights):
    dens_total = jnp.zeros((ORDER, WIDTH), jnp.float32)
    diag_total = jnp.zeros((WIDTH, WIDTH), jnp.float32)
    mask_bf = mask_rows.astype(jnp.bfloat16)[:, None, :, None]
    for pole_index in range(POLES):
        masked = (inv_block[pole_index].reshape(NBLK, BLOCK, NBLK, BLOCK) * mask_bf).reshape(ORDER, ORDER)
        product = jnp.dot(masked, factor[pole_index], preferred_element_type=jnp.float32)
        inner_term = jnp.dot(factor[pole_index].astype(jnp.float32).T, product, precision=lax.Precision.HIGHEST)
        dens_total = dens_total + weights[pole_index] * product
        diag_total = diag_total + weights[pole_index] * (diag_inv[pole_index].astype(jnp.float32) - inner_term)
    return (dens_total, diag_total)

def reference(inv_block, block_masks, panel_first, panel_second, diag_inverse, weights):
    dens_first, diag_first = supernode(inv_block, block_masks[0], panel_first, diag_inverse[0], weights)
    col_scale = jnp.sqrt(lax.optimization_barrier(jnp.mean(dens_first * dens_first, axis=0)) + 1e-06)
    rescaled = (panel_second / col_scale).astype(jnp.bfloat16)
    dens_second, diag_second = supernode(inv_block, block_masks[1], rescaled, diag_inverse[1], weights)
    return (jnp.stack([dens_first, dens_second]).astype(jnp.bfloat16), jnp.stack([diag_first, diag_second]))
```

```python
import functools

import jax
import jax.numpy as jnp
from jax import lax
from jax.experimental import pallas as pl
from jax.experimental.pallas import tpu as pltpu
from jax.sharding import PartitionSpec as P

CORES = 2
CHUNKS = 2


def shift(x, axis, step):
    size = lax.axis_size(axis)
    return lax.ppermute(x, axis, [(i, (i + step) % size) for i in range(size)])


def swap_core(x):
    size = lax.axis_size("col")
    return lax.ppermute(x, "col", [(i, i ^ 1) for i in range(size)])


def shift_z(x, step):
    size = lax.axis_size("col") // CORES
    pairs = [(i, ((i // CORES + step) % size) * CORES + i % CORES) for i in range(size * CORES)]
    return lax.ppermute(x, "col", pairs)


def after(x, *deps):
    return lax.optimization_barrier((x,) + deps)[0]


def product_kernel(zs, where_ref, weight_ref, a_ref, mask_ref, own_ref, recv_ref, away_ref, here_ref, f_ref):
    step = pl.program_id(0)

    @pl.when(jnp.logical_and(step == 0, where_ref[2] == 1))
    def _():
        f_ref[...] = own_ref[...]

    @pl.when(jnp.logical_and(step == 0, where_ref[2] == 0))
    def _():
        f_ref[...] = recv_ref[...]

    rows, cols = a_ref.shape
    groups = mask_ref.shape[1]
    shaped = a_ref[...].reshape(groups, rows // groups, cols)
    masked = (shaped * mask_ref[0][:, None, :]).reshape(rows, cols)
    part = jnp.dot(masked, f_ref[...], preferred_element_type=jnp.float32) * weight_ref[0]

    @pl.when(step < zs)
    def _():
        away_ref[...] = part.astype(away_ref.dtype)

    @pl.when(step >= zs)
    def _():
        here_ref[...] = part


def product(inverse, mask, own, recv, place, weight, n_pole):
    rows, cols = inverse.shape
    width = own.shape[1]
    blocks, groups, _ = mask.shape
    zs = blocks // (CORES * n_pole)
    block = rows // blocks

    def block_of(i, where):
        core = jnp.where(i < zs, 1 - where[0], where[0])
        return (lax.rem(i, zs) * CORES + core) * n_pole + where[1]

    return pl.pallas_call(
        functools.partial(product_kernel, zs),
        out_shape=(
            jax.ShapeDtypeStruct((zs * block, width), jnp.bfloat16),
            jax.ShapeDtypeStruct((zs * block, width), jnp.float32),
        ),
        grid_spec=pltpu.PrefetchScalarGridSpec(
            num_scalar_prefetch=1,
            grid=(CORES * zs,),
            in_specs=[
                pl.BlockSpec(memory_space=pltpu.SMEM),
                pl.BlockSpec((block, cols), lambda i, w: (block_of(i, w), 0)),
                pl.BlockSpec((1, groups, cols), lambda i, w: (block_of(i, w), 0, 0)),
                pl.BlockSpec((cols, width), lambda i, w: (0, 0)),
                pl.BlockSpec((cols, width), lambda i, w: (0, 0)),
            ],
            out_specs=(
                pl.BlockSpec((block, width), lambda i, w: (jnp.minimum(i, zs - 1), 0)),
                pl.BlockSpec((block, width), lambda i, w: (jnp.maximum(i - zs, 0), 0)),
            ),
            scratch_shapes=[pltpu.VMEM((cols, width), jnp.bfloat16)],
        ),
        compiler_params=pltpu.CompilerParams(vmem_limit_bytes=40 * 2**20),
        cost_estimate=pl.CostEstimate(
            flops=2 * CORES * zs * block * cols * width,
            bytes_accessed=2 * CORES * zs * block * cols + 6 * zs * block * width + 4 * cols * width,
            transcendentals=0,
        ),
    )(place, weight, inverse, mask, own, recv)


def sum_axes(x):
    x = x + swap_core(x)
    for axis in ("row", "pole"):
        x = x + sum(shift(x, axis, d) for d in range(1, lax.axis_size(axis)))
    return x + sum(shift_z(x, d) for d in range(1, lax.axis_size("col") // CORES))


def pick(x, index, axis):
    return lax.dynamic_index_in_dim(x, index, axis, keepdims=False)


def scatter_diag(term, diag, weight, ids):
    row, z, core, pole = ids
    n_row, n_pole = lax.axis_size("row"), lax.axis_size("pole")
    zs = lax.axis_size("col") // CORES
    size, width = term.shape
    split = (n_row, zs, CORES, n_pole, size // (n_row * zs * CORES * n_pole), width)
    term = term.reshape(split)
    send = pick(term, 1 - core, 2).astype(jnp.bfloat16)
    term = pick(term, core, 2) + swap_core(send)
    sends = [pick(term, (row + d) % n_row, 0).astype(jnp.bfloat16) for d in range(1, n_row)]
    term = pick(term, row, 0) + sum(shift(s, "row", d + 1).astype(jnp.float32) for d, s in enumerate(sends))
    sends = [pick(term, (z + d) % zs, 0).astype(jnp.bfloat16) for d in range(1, zs)]
    term = pick(term, z, 0) + sum(shift_z(s, d + 1).astype(jnp.float32) for d, s in enumerate(sends))
    base = pick(pick(pick(diag.reshape(split), row, 0), z, 0), core, 0).astype(jnp.float32) * weight
    both = jnp.stack([base, term], axis=1)
    sends = [pick(both, (pole + d) % n_pole, 0) for d in range(1, n_pole)]
    both = pick(both, pole, 0) + sum(shift(s, "pole", d + 1) for d, s in enumerate(sends))
    return both[0], both[1]


def gather_diag(piece):
    return lax.all_gather(piece.astype(jnp.bfloat16), ("row", "col", "pole"), axis=0, tiled=True).astype(jnp.float32)


def body(inv_block, block_masks, panel_first, panel_second, diag_inverse, weights):
    n_row, n_col, n_pole = (lax.axis_size(a) for a in ("row", "col", "pole"))
    row, col, pole = (lax.axis_index(a) for a in ("row", "col", "pole"))
    zs = n_col // CORES
    z, core = col // CORES, col % CORES
    inverse, weight = inv_block[0], weights[0]
    rows, cols = inverse.shape
    width = panel_first.shape[2]
    piece = width // CHUNKS
    blocks = n_col * n_pole
    block = rows // blocks
    ratio = n_col // n_row
    owner = col // ratio
    panels = (panel_first[0], panel_second[0])
    grain = rows // block_masks.shape[1]
    groups = max(1, block // grain)
    fine = block // groups
    mask = jnp.repeat(block_masks.astype(jnp.bfloat16), grain // fine, axis=1)
    mask = jnp.repeat(mask, grain, axis=2).reshape(2, blocks, groups, cols)
    mine = (row == owner).astype(jnp.int32)

    order = [(k, n) for k in range(2) for n in range(CHUNKS)]
    own, got = {}, {}
    last = None
    for k, n in order:
        start = (col % ratio) * cols
        src = lax.dynamic_slice(panels[k], (start, n * piece), (cols, piece))
        own[k, n] = src
        if last is not None:
            src = after(src, last)
        total = None
        for d in range(1, n_row):
            pairs = []
            for j in range(n_col):
                first = j // ratio
                pairs.append((first * n_col + j, ((first + d) % n_row) * n_col + j))
            arrived = lax.ppermute(src, ("row", "col"), pairs)
            total = arrived if total is None else total + arrived
        got[k, n] = src if total is None else total
        last = got[k, n]

    weight_arr = weights.reshape(1)
    local = [p.reshape(zs, CORES, n_pole, block, width) for p in panels]

    def rows_of(k, dest):
        picked = pick(pick(local[k], core, 1), dest, 1)
        return picked.reshape(zs * block, width)

    finals, terms = {}, {}
    for k, n in order:
        merged, arrived = {}, []
        for d in list(range(1, n_pole)) + [0]:
            dest = (pole + d) % n_pole
            place = jnp.stack([core, dest, mine]).astype(jnp.int32)
            away, here = product(inverse, mask[k], own[k, n], got[k, n], place, weight_arr, n_pole)
            merged[d] = here + swap_core(away).astype(jnp.float32)
            if d > 0:
                arrived.append(shift(merged[d].astype(jnp.bfloat16), "pole", d))
        term = 0.0
        for d in range(n_pole):
            term = term + lax.dot_general(
                rows_of(k, (pole + d) % n_pole), merged[d].astype(jnp.bfloat16),
                (((0,), (0,)), ((), ())), preferred_element_type=jnp.float32,
            )
        terms[k, n] = -term
        total = merged[0] + sum(a.astype(jnp.float32) for a in arrived)
        total = total.reshape(zs, block, piece)
        sends = [pick(total, (z + d) % zs, 0).astype(jnp.bfloat16) for d in range(1, zs)]
        final = pick(total, z, 0)
        for d, s in enumerate(sends):
            final = final + shift_z(s, d + 1).astype(jnp.float32)
        finals[k, n] = final

    dens = [jnp.concatenate([finals[k, n] for n in range(CHUNKS)], axis=1) for k in range(2)]
    squares = sum_axes(jnp.sum(dens[0] * dens[0], axis=0))
    scale = jnp.sqrt(squares / (rows * n_row) + 1e-06)
    out = jnp.stack([dens[0].astype(jnp.bfloat16), (dens[1] / scale).astype(jnp.bfloat16)])

    ids = (row, z, core, pole)
    pieces = []
    for k in range(2):
        term = jnp.concatenate([terms[k, n] for n in range(CHUNKS)], axis=1)
        base, inner = scatter_diag(term, diag_inverse[k, 0], weight, ids)
        if k == 1:
            index = ((row * n_col + col) * n_pole + pole) * base.shape[0]
            inner = inner / (lax.dynamic_slice(scale, (index,), (base.shape[0],))[:, None] * scale)
        pieces.append(gather_diag(base + inner))
    return out, jnp.stack(pieces)


def solution(mesh):
    placed = (
        P("pole", "row", "col"),
        P(None, "row", "col"),
        P("pole", "row", None),
        P("pole", "row", None),
        P(None, "pole", None, None),
        P("pole"),
    )
    return jax.shard_map(
        body,
        mesh=mesh,
        in_specs=placed,
        out_specs=(P(None, ("row", "col", "pole"), None), P()),
        check_vma=False,
    )
```

```python
import functools

import jax
import jax.numpy as jnp
from jax import lax
from jax.experimental import pallas as pl
from jax.experimental.pallas import tpu as pltpu
from jax.sharding import PartitionSpec as P

CORES = 2
PACK = 16
PARTS = ((0, 0, 2), (0, 2, 2), (1, 0, 2), (1, 2, 2))


def swap(x, axis, mask):
    size = lax.axis_size(axis)
    return lax.ppermute(x, axis, [(i, i ^ mask) for i in range(size)])


def swap_core(x, mask=1):
    return swap(x, "col", mask)


def swap_z(x, mask):
    return swap(x, "col", mask * CORES)


def swap_row(x, mask):
    return swap(x, "row", mask)


def swap_pole(x, mask):
    return swap(x, "pole", mask)


def after(x, *deps):
    if not deps:
        return x
    return lax.optimization_barrier((x,) + deps)[0]


def pick(x, index, axis):
    return lax.dynamic_index_in_dim(x, index, axis, keepdims=False)


def halve_step(sources, axis, index, bit, kind):
    size = sources[0].shape[axis]
    low = (index >> bit) & 1
    send, keep = 0.0, 0.0
    for x in sources:
        pairs = x.reshape(x.shape[:axis] + (size // 2, 2) + x.shape[axis + 1:])
        send = send + pick(pairs, 1 - low, axis + 1).astype(jnp.float32)
        keep = keep + pick(pairs, low, axis + 1).astype(jnp.float32)
    return send.astype(kind), keep


def halve(x, axis, index, exchange, kind):
    sources, bit = [x], 0
    while sources[0].shape[axis] > 1:
        send, keep = halve_step(sources, axis, index, bit, kind)
        sources = [keep, exchange(send, 1 << bit)]
        bit += 1
    x = sum(y.astype(jnp.float32) for y in sources)
    return x.reshape(x.shape[:axis] + x.shape[axis + 1:])


class ZSum:
    def __init__(self, sources, z):
        self.sources, self.z, self.bit = sources, z, 0

    def step(self):
        send, keep = halve_step(self.sources, 0, self.z, self.bit, jnp.bfloat16)
        self.sources = [keep, swap_z(send, 1 << self.bit)]
        self.bit += 1
        return send, keep

    def done(self):
        return self.sources[0].shape[0] == 1

    def result(self):
        x = sum(y.astype(jnp.float32) for y in self.sources)
        return x.reshape(x.shape[1:])


def double(x, axis, index, size, exchange):
    x = jnp.expand_dims(x, axis)
    bits = size.bit_length() - 1
    for bit in reversed(range(bits)):
        other = exchange(x, 1 << bit)
        low = (index >> bit) & 1
        both = jnp.where(low == 0, jnp.stack([x, other], axis + 1), jnp.stack([other, x], axis + 1))
        x = both.reshape(x.shape[:axis] + (2 * x.shape[axis],) + x.shape[axis + 1:])
    return x


def masked_product(a_ref, mask_ref, f_ref, weight_ref):
    rows, cols = a_ref.shape
    groups = mask_ref.shape[1]
    shaped = a_ref[...].reshape(groups, rows // (groups * PACK), PACK, cols)
    masked = (shaped * mask_ref[0][:, None]).reshape(rows, cols)
    return jnp.dot(masked, f_ref[...], preferred_element_type=jnp.float32) * weight_ref[0]


def away_kernel(where_ref, weight_ref, a_ref, mask_ref, f_ref, out_ref):
    out_ref[...] = masked_product(a_ref, mask_ref, f_ref, weight_ref).astype(out_ref.dtype)


def here_kernel(pieces, where_ref, weight_ref, a_ref, mask_ref, f_ref, recv_ref, panel_ref, start_ref, *outs):
    total = masked_product(a_ref, mask_ref, f_ref, weight_ref) + recv_ref[...].astype(jnp.float32)
    width = total.shape[1] // pieces
    for n in range(pieces):
        outs[n][...] = total[:, n * width:(n + 1) * width].astype(outs[n].dtype)
    term = lax.dot_general(
        panel_ref[...], total.astype(jnp.bfloat16), (((0,), (0,)), ((), ())), preferred_element_type=jnp.float32
    )
    term_ref = outs[pieces]

    @pl.when(pl.program_id(0) == 0)
    def _():
        term_ref[...] = start_ref[...] - term

    @pl.when(pl.program_id(0) > 0)
    def _():
        term_ref[...] = term_ref[...] - term


def product(inverse, mask, factor, place, weight, n_pole, merge=None):
    cols = inverse.shape[1]
    width = factor.shape[1]
    blocks, groups = mask.shape[:2]
    zs = blocks // (CORES * n_pole)
    block = inverse.shape[0] // blocks

    def block_of(i, where):
        return (i * CORES + where[0]) * n_pole + where[1]

    in_specs = [
        pl.BlockSpec(memory_space=pltpu.SMEM),
        pl.BlockSpec((block, cols), lambda i, w: (block_of(i, w), 0)),
        pl.BlockSpec((1, groups, PACK, cols), lambda i, w: (block_of(i, w), 0, 0, 0)),
        pl.BlockSpec((cols, width), lambda i, w: (0, 0)),
    ]
    flops = 2 * zs * block * cols
    nbytes = zs * block * width
    if merge is None:
        kernel, extra = away_kernel, ()
        out_shape = jax.ShapeDtypeStruct((zs * block, width), jnp.bfloat16)
        out_specs = pl.BlockSpec((block, width), lambda i, w: (i, 0))
    else:
        recv, panel, start, pieces, kind = merge
        extra = (recv, panel, start)
        kernel = functools.partial(here_kernel, pieces)
        full = panel.shape[1]
        in_specs += [
            pl.BlockSpec((block, width), lambda i, w: (i, 0)),
            pl.BlockSpec((block, full), lambda i, w: (block_of(i, w), 0)),
            pl.BlockSpec((full, width), lambda i, w: (0, 0)),
        ]
        piece = width // pieces
        out_shape = [jax.ShapeDtypeStruct((zs * block, piece), kind)] * pieces
        out_shape.append(jax.ShapeDtypeStruct((full, width), jnp.float32))
        out_specs = [pl.BlockSpec((block, piece), lambda i, w: (i, 0))] * pieces
        out_specs.append(pl.BlockSpec((full, width), lambda i, w: (0, 0)))
    return pl.pallas_call(
        kernel,
        out_shape=out_shape,
        grid_spec=pltpu.PrefetchScalarGridSpec(
            num_scalar_prefetch=1, grid=(zs,), in_specs=in_specs, out_specs=out_specs
        ),
        compiler_params=pltpu.CompilerParams(vmem_limit_bytes=40 * 2**20),
        cost_estimate=pl.CostEstimate(flops=flops, bytes_accessed=nbytes, transcendentals=0),
    )(place, weight, inverse, mask, factor, *extra)


def fetch_factor(panel, first, width, ids, last):
    row, col, cols = ids
    n_row, n_col = lax.axis_size("row"), lax.axis_size("col")
    zs = n_col // CORES
    ratio = n_col // n_row

    def mirror(j):
        return (zs - 1 - j // CORES) * CORES + j % CORES

    far = cols * 5 // 16 if n_row == 2 and zs > 1 else 0
    near = cols - far
    start = (col % ratio) * cols
    own = lax.dynamic_slice(panel, (start, first), (cols, width))
    parts = [(own[:near], lambda j: j)]
    if far > 0:
        other = (mirror(col) % ratio) * cols + near
        parts.append((lax.dynamic_slice(panel, (other, first), (far, width)), mirror))
    got = []
    for src, source in parts:
        if last is not None:
            src = after(src, *last)
        total = None
        for d in range(1, n_row):
            pairs = []
            for j in range(n_col):
                owner = j // ratio
                pairs.append((owner * n_col + source(j), ((owner + d) % n_row) * n_col + j))
            arrived = lax.ppermute(src, ("row", "col"), pairs)
            total = arrived if total is None else total + arrived
        got.append(src if total is None else total)
    return own, got


def body(inv_block, block_masks, panel_first, panel_second, diag_inverse, weights):
    n_row, n_col, n_pole = (lax.axis_size(a) for a in ("row", "col", "pole"))
    row, col, pole = (lax.axis_index(a) for a in ("row", "col", "pole"))
    zs = n_col // CORES
    z, core = col // CORES, col % CORES
    inverse, weight = inv_block[0], weights[0]
    rows, cols = inverse.shape
    width = panel_first.shape[2]
    quarter = width // 4
    blocks = n_col * n_pole
    block = rows // blocks
    panels = (panel_first[0], panel_second[0])
    grain = rows // block_masks.shape[1]
    groups = max(1, block // grain)
    fine = block // groups

    fetched, last = [], None
    for k, first, size in PARTS:
        own, last = fetch_factor(panels[k], first * quarter, size * quarter, (row, col, cols), last)
        fetched.append((own, last))
    mine = row == col // (n_col // n_row)

    masks = []
    for k in range(2):
        mask = jnp.repeat(block_masks[k].astype(jnp.bfloat16), grain // fine, axis=0)
        mask = jnp.repeat(mask, grain, axis=1).reshape(blocks, groups, 1, cols)
        masks.append(jnp.broadcast_to(mask, (blocks, groups, PACK, cols)))
    got, *masks = lax.optimization_barrier((fetched[0][1], *masks))
    fetched[0] = (fetched[0][0], got)

    def take(part, *deps):
        own, got = fetched[part]
        return jnp.where(mine, own, after(jnp.concatenate(got, axis=0), *deps))

    def place(c, d, *deps):
        return after(jnp.stack([c, (pole + d) % n_pole]).astype(jnp.int32), *deps)

    dests = list(range(1, n_pole)) + [0]
    factor = take(0)
    token = ()
    units = []
    terms = [[], []]
    for part, (k, first, size) in enumerate(PARTS):
        wide = size * quarter
        pieces = max(1, size // 2)
        received = {}
        for d in dests:
            away = product(inverse, masks[k], factor, place(1 - core, d, *token), weights, n_pole)
            token = (away,)
            received[d] = swap_core(away)
        term = jnp.zeros((width, wide), jnp.float32)
        arrived = [[] for _ in range(pieces)]
        upcoming = None
        final = part + 1 == len(PARTS)
        for d in sorted(dests) if final else dests:
            if d == 0:
                if not final:
                    upcoming = take(part + 1, *token)
                    token += (upcoming,)
                for unit in units:
                    if not unit.done():
                        token += unit.step()
            kind = jnp.bfloat16 if d > 0 else jnp.float32
            *out, term = product(
                inverse, masks[k], factor, place(core, d, *token), weights, n_pole,
                (received[d], panels[k], term, pieces, kind),
            )
            token = (out[0],)
            if d == 0:
                sums = out
            else:
                pairs = [(i, (i + d) % n_pole) for i in range(n_pole)]
                before = ()
                for n in range(pieces):
                    came = lax.ppermute(after(out[n], *before), "pole", pairs)
                    before = (came,)
                    arrived[n].append(came)
        terms[k].append(term)
        factor = upcoming
        for n in range(pieces):
            sources = [x.reshape(zs, block, x.shape[1]) for x in [sums[n]] + arrived[n]]
            units.append(ZSum(sources, z))
            units[-1].k = k
    finals, gate = [[], []], ()
    for unit in units:
        while not unit.done():
            sent = unit.step()
            if unit is units[-2] or unit.bit == 1:
                gate = gate[:2] + sent
        finals[unit.k].append(unit.result())

    dens = [jnp.concatenate(f, axis=1) for f in finals]
    squares = jnp.sum(dens[0] * dens[0], axis=0)
    for exchange, size in ((swap_core, CORES), (swap_row, n_row), (swap_z, zs), (swap_pole, n_pole)):
        for bit in range(size.bit_length() - 1):
            squares = squares + exchange(squares, 1 << bit)
    scale = jnp.sqrt(squares / (rows * n_row) + 1e-06)
    out = jnp.stack([dens[0].astype(jnp.bfloat16), (dens[1] / scale).astype(jnp.bfloat16)])

    each = width // (n_row * blocks)
    split = (2, n_row, zs, CORES, n_pole, each, width)
    term = jnp.stack([jnp.concatenate(t, axis=1) for t in terms]).reshape(split)
    term = halve(term, 3, core, swap_core, jnp.bfloat16)
    term = halve(term, 1, row, swap_row, jnp.bfloat16)
    term = halve(term, 1, z, swap_z, jnp.bfloat16)
    base = pick(pick(pick(diag_inverse.reshape(split), core, 3), row, 1), z, 1).astype(jnp.float32) * weight
    both = halve(jnp.stack([base, term]), 2, pole, swap_pole, jnp.float32)
    base, term = both[0], both[1]
    index = ((row * n_col + col) * n_pole + pole) * each
    inner = term[1] / (lax.dynamic_slice(scale, (index,), (each,))[:, None] * scale)
    piece = (base + jnp.stack([term[0], inner])).astype(jnp.bfloat16)
    piece = double(after(piece, *gate), 1, pole, n_pole, swap_pole)
    piece = double(piece, 1, z, zs, swap_z)
    piece = double(piece, 1, row, n_row, swap_row)
    piece = double(piece, 3, core, CORES, swap_core)
    return out, piece.reshape(2, width, width).astype(jnp.float32)


def solution(mesh):
    placed = (
        P("pole", "row", "col"),
        P(None, "row", "col"),
        P("pole", "row", None),
        P("pole", "row", None),
        P(None, "pole", None, None),
        P("pole"),
    )
    return jax.shard_map(
        body,
        mesh=mesh,
        in_specs=placed,
        out_specs=(P(None, ("row", "col", "pole"), None), P()),
        check_vma=False,
    )
```

```python
import functools

import jax
import jax.numpy as jnp
from jax import lax
from jax.experimental import pallas as pl
from jax.experimental.pallas import tpu as pltpu
from jax.sharding import PartitionSpec as P

CORES = 2
PACK = 16
AWAY = 2
PARTS = ((0, 0, 4, 1), (1, 0, 4, 2))


def swap(x, axis, mask):
    size = lax.axis_size(axis)
    return lax.ppermute(x, axis, [(i, i ^ mask) for i in range(size)])


def swap_core(x, mask=1):
    return swap(x, "col", mask)


def swap_z(x, mask):
    return swap(x, "col", mask * CORES)


def swap_row(x, mask):
    return swap(x, "row", mask)


def swap_pole(x, mask):
    return swap(x, "pole", mask)


def after(x, *deps):
    if not deps:
        return x
    return lax.optimization_barrier((x,) + deps)[0]


def pick(x, index, axis):
    return lax.dynamic_index_in_dim(x, index, axis, keepdims=False)


def halve_step(sources, axis, index, bit, kind):
    size = sources[0].shape[axis]
    low = (index >> bit) & 1
    send, keep = 0.0, 0.0
    for x in sources:
        pairs = x.reshape(x.shape[:axis] + (size // 2, 2) + x.shape[axis + 1:])
        send = send + pick(pairs, 1 - low, axis + 1).astype(jnp.float32)
        keep = keep + pick(pairs, low, axis + 1).astype(jnp.float32)
    return send.astype(kind), keep


def halve(x, axis, index, exchange, kind, before_last=()):
    sources, bit = [x], 0
    while sources[0].shape[axis] > 1:
        if sources[0].shape[axis] == 2:
            sources[0] = after(sources[0], *before_last)
        send, keep = halve_step(sources, axis, index, bit, kind)
        sources = [keep, exchange(send, 1 << bit)]
        bit += 1
    x = sum(y.astype(jnp.float32) for y in sources)
    return x.reshape(x.shape[:axis] + x.shape[axis + 1:])


class ZSum:
    def __init__(self, sources, z):
        self.sources, self.z, self.bit = sources, z, 0

    def step(self):
        send, keep = halve_step(self.sources, 0, self.z, self.bit, jnp.bfloat16)
        self.sources = [keep, swap_z(send, 1 << self.bit)]
        self.bit += 1
        return send, keep

    def done(self):
        return self.sources[0].shape[0] == 1

    def result(self):
        x = sum(y.astype(jnp.float32) for y in self.sources)
        return x.reshape(x.shape[1:])


def double(x, axis, index, size, exchange):
    x = jnp.expand_dims(x, axis)
    bits = size.bit_length() - 1
    for bit in reversed(range(bits)):
        other = exchange(x, 1 << bit)
        low = (index >> bit) & 1
        both = jnp.where(low == 0, jnp.stack([x, other], axis + 1), jnp.stack([other, x], axis + 1))
        x = both.reshape(x.shape[:axis] + (2 * x.shape[axis],) + x.shape[axis + 1:])
    return x


def masked_product(a_ref, mask_ref, f_ref, weight_ref):
    rows, cols = a_ref.shape
    groups = mask_ref.shape[1]
    shaped = a_ref[...].reshape(groups, rows // (groups * PACK), PACK, cols)
    masked = (shaped * mask_ref[0][:, None]).reshape(rows, cols)
    return jnp.dot(masked, f_ref[...], preferred_element_type=jnp.float32) * weight_ref[0]


def away_kernel(where_ref, weight_ref, a_ref, mask_ref, f_ref, *outs):
    total = masked_product(a_ref, mask_ref, f_ref, weight_ref)
    width = total.shape[1] // len(outs)
    for n, out_ref in enumerate(outs):
        out_ref[...] = total[:, n * width:(n + 1) * width].astype(out_ref.dtype)


def here_kernel(pieces, where_ref, weight_ref, a_ref, mask_ref, f_ref, panel_ref, start_ref, *refs):
    recvs, outs = refs[:AWAY], refs[AWAY:]
    total = masked_product(a_ref, mask_ref, f_ref, weight_ref)
    total = total + jnp.concatenate([r[...].astype(jnp.float32) for r in recvs], axis=1)
    width = total.shape[1] // pieces
    for n in range(pieces):
        outs[n][...] = total[:, n * width:(n + 1) * width].astype(outs[n].dtype)
    term = lax.dot_general(
        panel_ref[...], total.astype(jnp.bfloat16), (((0,), (0,)), ((), ())), preferred_element_type=jnp.float32
    )
    term_ref = outs[pieces]

    @pl.when(pl.program_id(0) == 0)
    def _():
        term_ref[...] = start_ref[...] - term

    @pl.when(pl.program_id(0) > 0)
    def _():
        term_ref[...] = term_ref[...] - term


def product(inverse, mask, factor, place, weight, n_pole, merge=None):
    cols = inverse.shape[1]
    width = factor.shape[1]
    blocks, groups = mask.shape[:2]
    zs = blocks // (CORES * n_pole)
    block = inverse.shape[0] // blocks

    def block_of(i, where):
        return (i * CORES + where[0]) * n_pole + where[1]

    in_specs = [
        pl.BlockSpec(memory_space=pltpu.SMEM),
        pl.BlockSpec((block, cols), lambda i, w: (block_of(i, w), 0)),
        pl.BlockSpec((1, groups, PACK, cols), lambda i, w: (block_of(i, w), 0, 0, 0)),
        pl.BlockSpec((cols, width), lambda i, w: (0, 0)),
    ]
    flops = 2 * zs * block * cols
    nbytes = zs * block * width
    if merge is None:
        kernel, extra = away_kernel, ()
        part = width // AWAY
        out_shape = [jax.ShapeDtypeStruct((zs * block, part), jnp.bfloat16)] * AWAY
        out_specs = [pl.BlockSpec((block, part), lambda i, w: (i, 0))] * AWAY
    else:
        recv, panel, start, pieces, kind = merge
        extra = (panel, start, *recv)
        kernel = functools.partial(here_kernel, pieces)
        full = panel.shape[1]
        in_specs += [
            pl.BlockSpec((block, full), lambda i, w: (block_of(i, w), 0)),
            pl.BlockSpec((full, width), lambda i, w: (0, 0)),
        ] + [pl.BlockSpec((block, width // AWAY), lambda i, w: (i, 0))] * AWAY
        piece = width // pieces
        out_shape = [jax.ShapeDtypeStruct((zs * block, piece), kind)] * pieces
        out_shape.append(jax.ShapeDtypeStruct((full, width), jnp.float32))
        out_specs = [pl.BlockSpec((block, piece), lambda i, w: (i, 0))] * pieces
        out_specs.append(pl.BlockSpec((full, width), lambda i, w: (0, 0)))
    return pl.pallas_call(
        kernel,
        out_shape=out_shape,
        grid_spec=pltpu.PrefetchScalarGridSpec(
            num_scalar_prefetch=1, grid=(zs,), in_specs=in_specs, out_specs=out_specs
        ),
        compiler_params=pltpu.CompilerParams(vmem_limit_bytes=40 * 2**20),
        cost_estimate=pl.CostEstimate(flops=flops, bytes_accessed=nbytes, transcendentals=0),
    )(place, weight, inverse, mask, factor, *extra)


def fetch_factor(panel, first, width, ids, last):
    row, col, cols = ids
    n_row, n_col = lax.axis_size("row"), lax.axis_size("col")
    ratio = n_col // n_row
    start = (col % ratio) * cols
    own = lax.dynamic_slice(panel, (start, first), (cols, width))
    src = after(own, *last)
    got = None
    for d in range(1, n_row):
        pairs = [((j // ratio) * n_col + j, ((j // ratio + d) % n_row) * n_col + j) for j in range(n_col)]
        arrived = lax.ppermute(src, ("row", "col"), pairs)
        got = arrived if got is None else got + arrived
    return own, own if got is None else got


def body(inv_block, block_masks, panel_first, panel_second, diag_inverse, weights):
    n_row, n_col, n_pole = (lax.axis_size(a) for a in ("row", "col", "pole"))
    row, col, pole = (lax.axis_index(a) for a in ("row", "col", "pole"))
    zs = n_col // CORES
    z, core = col // CORES, col % CORES
    inverse, weight = inv_block[0], weights[0]
    rows, cols = inverse.shape
    width = panel_first.shape[2]
    quarter = width // 4
    blocks = n_col * n_pole
    block = rows // blocks
    panels = (panel_first[0], panel_second[0])
    grain = rows // block_masks.shape[1]
    groups = max(1, block // grain)
    fine = block // groups

    fetched, last = [], ()
    for k, first, size, _ in PARTS:
        own, last = fetch_factor(panels[k], first * quarter, size * quarter, (row, col, cols), last)
        fetched.append((own, last))
        last = (last,)
    mine = row == col // (n_col // n_row)

    masks = []
    for k in range(2):
        mask = jnp.repeat(block_masks[k].astype(jnp.bfloat16), grain // fine, axis=0)
        mask = jnp.repeat(mask, grain, axis=1).reshape(blocks, groups, 1, cols)
        masks.append(jnp.broadcast_to(mask, (blocks, groups, PACK, cols)))
    got, *masks = lax.optimization_barrier((fetched[0][1], *masks))
    fetched[0] = (fetched[0][0], got)

    def take(part, *deps):
        own, got = fetched[part]
        return jnp.where(mine, own, after(got, *deps))

    def place(c, d, *deps):
        return after(jnp.stack([c, (pole + d) % n_pole]).astype(jnp.int32), *deps)

    dests = list(range(1, n_pole)) + [0]
    factor = take(0)
    token = ()
    units = []
    terms = [[], []]
    for part, (k, first, size, pieces) in enumerate(PARTS):
        wide = size * quarter
        received = {}
        for d in dests:
            away = product(inverse, masks[k], factor, place(1 - core, d, *token), weights, n_pole)
            token = (away[0],)
            received[d] = [swap_core(x) for x in away]
        term = jnp.zeros((width, wide), jnp.float32)
        arrived = [[] for _ in range(pieces)]
        final = part + 1 == len(PARTS)
        for d in dests:
            if d == 0:
                for unit in units:
                    if not unit.done():
                        token += unit.step()
            kind = jnp.bfloat16 if d > 0 else jnp.float32
            *out, term = product(
                inverse, masks[k], factor, place(core, d, *token), weights, n_pole,
                (received[d], panels[k], term, pieces, kind),
            )
            token = (out[0],)
            if d == 0:
                sums = out
            else:
                pairs = [(i, (i + d) % n_pole) for i in range(n_pole)]
                before = ()
                for n in range(pieces):
                    came = lax.ppermute(after(out[n], *before), "pole", pairs)
                    before = (came,)
                    arrived[n].append(came)
        terms[k].append(term)
        if not final:
            factor = take(part + 1, *token)
        for n in range(pieces):
            sources = [x.reshape(zs, block, x.shape[1]) for x in [sums[n]] + arrived[n]]
            units.append(ZSum(sources, z))
            units[-1].k = k
    first, second, third = (), (), ()
    for unit in units[:-1]:
        if not unit.done():
            first += unit.step()
    second = units[-1].step()
    for unit in units[:-1]:
        while not unit.done():
            second += unit.step()
    while not units[-1].done():
        third = units[-1].step()
    finals = [[], []]
    for unit in units:
        finals[unit.k].append(unit.result())
    second += tuple(finals[0])

    dens = [jnp.concatenate(f, axis=1) for f in finals]
    squares = jnp.sum(dens[0] * dens[0], axis=0)
    for exchange, size in ((swap_core, CORES), (swap_row, n_row), (swap_z, zs), (swap_pole, n_pole)):
        for bit in range(size.bit_length() - 1):
            squares = squares + exchange(squares, 1 << bit)
    scale = jnp.sqrt(squares / (rows * n_row) + 1e-06)
    out = jnp.stack([dens[0].astype(jnp.bfloat16), (dens[1] / scale).astype(jnp.bfloat16)])

    each = width // (n_row * blocks)
    split = (2, n_row, zs, CORES, n_pole, each, width)
    term = jnp.stack([jnp.concatenate(t, axis=1) for t in terms]).reshape(split)
    term = halve(term, 3, core, swap_core, jnp.bfloat16)
    term = halve(after(term, *first), 1, row, swap_row, jnp.bfloat16)
    term = halve(term, 1, z, swap_z, jnp.bfloat16, second)
    base = pick(pick(pick(diag_inverse.reshape(split), core, 3), row, 1), z, 1).astype(jnp.float32) * weight
    both = halve(jnp.stack([base, term]), 2, pole, swap_pole, jnp.float32)
    piece = jnp.concatenate([both[0] + both[1] * jnp.array([1, 0], jnp.float32)[:, None, None], both[1, 1:]])
    piece = double(piece.astype(jnp.bfloat16), 1, pole, n_pole, swap_pole)
    piece = double(after(piece, *third), 1, z, zs, swap_z)
    piece = double(after(piece, scale), 1, row, n_row, swap_row)
    piece = double(piece, 3, core, CORES, swap_core)
    piece = piece.reshape(3, width, width).astype(jnp.float32)
    scaled = piece[1] + piece[2] / (scale[:, None] * scale)
    return out, jnp.stack([piece[0], scaled])


def solution(mesh):
    placed = (
        P("pole", "row", "col"),
        P(None, "row", "col"),
        P("pole", "row", None),
        P("pole", "row", None),
        P(None, "pole", None, None),
        P("pole"),
    )
    return jax.shard_map(
        body,
        mesh=mesh,
        in_specs=placed,
        out_specs=(P(None, ("row", "col", "pole"), None), P()),
        check_vma=False,
    )
```

```python
import jax
import jax.numpy as jnp
from jax import lax
from jax.experimental import pallas as pl
from jax.experimental.pallas import tpu as pltpu
from jax.sharding import PartitionSpec as P

CORES = 2
AWAY = 2
CHUNKS = 2


def swap(x, axis, mask):
    size = lax.axis_size(axis)
    return lax.ppermute(x, axis, [(i, i ^ mask) for i in range(size)])


def swap_core(x, mask=1):
    return swap(x, "col", mask)


def swap_z(x, mask):
    return swap(x, "col", mask * CORES)


def swap_row(x, mask):
    return swap(x, "row", mask)


def swap_pole(x, mask):
    return swap(x, "pole", mask)


def after(x, *deps):
    if not deps:
        return x
    return lax.optimization_barrier((x,) + deps)[0]


def pick(x, index, axis):
    return lax.dynamic_index_in_dim(x, index, axis, keepdims=False)


def halve(x, axis, index, exchange, kind):
    bit = 0
    while x.shape[axis] > 1:
        size = x.shape[axis]
        pairs = x.reshape(x.shape[:axis] + (size // 2, 2) + x.shape[axis + 1:])
        low = (index >> bit) & 1
        send = pick(pairs, 1 - low, axis + 1).astype(kind)
        x = pick(pairs, low, axis + 1).astype(jnp.float32) + exchange(send, 1 << bit).astype(jnp.float32)
        bit += 1
    return x.reshape(x.shape[:axis] + x.shape[axis + 1:])


def split_three(x):
    terms = []
    for _ in range(3):
        high = lax.reduce_precision(x, 8, 7)
        terms.append(high.astype(jnp.bfloat16))
        x = x - high
    return jnp.stack(terms)


def double(x, squares, axis, index, bit, exchange):
    count = x.size // x.shape[-1]
    message = jnp.concatenate([x.reshape(count, x.shape[-1]), split_three(squares)])
    other = exchange(message, 1 << bit)
    squares = squares + jnp.sum(other[count:].astype(jnp.float32), axis=0)
    other = other[:count].reshape(x.shape)
    low = (index >> bit) & 1
    both = jnp.where(low == 0, jnp.stack([x, other], axis + 1), jnp.stack([other, x], axis + 1))
    return both.reshape(x.shape[:axis] + (2 * x.shape[axis],) + x.shape[axis + 1:]), squares


class ZSum:
    def __init__(self, sources, z):
        self.sources, self.z, self.bit = [(x, 0) for x in sources], z, 0
        self.bits = sources[0].shape[0].bit_length() - 1

    def part(self, flip, *deps):
        total = 0.0
        for x, depth in self.sources:
            spread = 1 << (self.bit - depth + flip)
            index = (self.z >> depth) & (spread - 1)
            if flip:
                index = index ^ (spread >> 1)
            x = x.reshape((x.shape[0] // spread, spread) + x.shape[1:])
            total = total + pick(after(x, *deps), index, 1).astype(jnp.float32)
        return total

    def step(self, *deps):
        send = self.part(1, *deps).astype(jnp.bfloat16)
        came = swap_z(send, 1 << self.bit)
        self.bit += 1
        self.sources.append((came, self.bit))
        return send

    def done(self):
        return self.bit == self.bits

    def result(self, *deps):
        x = self.part(0, *deps)
        return x.reshape(x.shape[1:])


def mask_kernel(a_ref, mask_ref, *outs):
    rows, cols = a_ref.shape
    groups = mask_ref.shape[2]
    shaped = a_ref[...].reshape(groups, rows // groups, cols)
    for k, out_ref in enumerate(outs):
        out_ref[...] = (shaped * mask_ref[k, 0][:, None, :]).reshape(rows, cols)


def apply_masks(inverse, mask):
    rows, cols = inverse.shape
    count, blocks, groups, _ = mask.shape
    block = rows // blocks
    spec = pl.BlockSpec((block, cols), lambda i: (i, 0))
    return pl.pallas_call(
        mask_kernel,
        out_shape=[jax.ShapeDtypeStruct((rows, cols), inverse.dtype)] * count,
        grid=(blocks,),
        in_specs=[spec, pl.BlockSpec((count, 1, groups, cols), lambda i: (0, i, 0, 0))],
        out_specs=[spec] * count,
        compiler_params=pltpu.CompilerParams(vmem_limit_bytes=40 * 2**20),
        cost_estimate=pl.CostEstimate(flops=2 * rows * cols, bytes_accessed=6 * rows * cols, transcendentals=0),
    )(inverse, mask)


def weighted_product(a_ref, f_ref, weight_ref):
    return jnp.dot(a_ref[...], f_ref[...], preferred_element_type=jnp.float32) * weight_ref[0]


def away_kernel(where_ref, weight_ref, a_ref, f_ref, *outs):
    total = weighted_product(a_ref, f_ref, weight_ref)
    width = total.shape[1] // len(outs)
    for n, out_ref in enumerate(outs):
        out_ref[...] = total[:, n * width:(n + 1) * width].astype(out_ref.dtype)


def here_kernel(where_ref, weight_ref, a_ref, f_ref, panel_ref, start_ref, *refs):
    recvs, (out_ref, term_ref) = refs[:AWAY], refs[AWAY:]
    total = weighted_product(a_ref, f_ref, weight_ref)
    total = total + jnp.concatenate([r[...].astype(jnp.float32) for r in recvs], axis=1)
    out_ref[...] = total.astype(out_ref.dtype)
    term = lax.dot_general(
        panel_ref[...], total.astype(jnp.bfloat16), (((0,), (0,)), ((), ())), preferred_element_type=jnp.float32
    )

    @pl.when(pl.program_id(0) == 0)
    def _():
        term_ref[...] = start_ref[...] - term

    @pl.when(pl.program_id(0) > 0)
    def _():
        term_ref[...] = term_ref[...] - term


def product(masked, factor, place, weight, sizes, merge=None):
    zs, block, n_pole = sizes
    cols = masked.shape[1]
    width = factor.shape[1]

    def block_of(i, where):
        return (i * CORES + where[0]) * n_pole + where[1]

    in_specs = [
        pl.BlockSpec(memory_space=pltpu.SMEM),
        pl.BlockSpec((block, cols), lambda i, w: (block_of(i, w), 0)),
        pl.BlockSpec((cols, width), lambda i, w: (0, 0)),
    ]
    part = [pl.BlockSpec((block, width // AWAY), lambda i, w: (i, 0))] * AWAY
    if merge is None:
        kernel, extra = away_kernel, ()
        out_shape = [jax.ShapeDtypeStruct((zs * block, width // AWAY), jnp.bfloat16)] * AWAY
        out_specs = part
    else:
        recv, panel, start, kind = merge
        kernel, extra = here_kernel, (panel, start, *recv)
        full = panel.shape[1]
        term = pl.BlockSpec((full, width), lambda i, w: (0, 0))
        in_specs += [pl.BlockSpec((block, full), lambda i, w: (block_of(i, w), 0)), term] + part
        out_shape = [jax.ShapeDtypeStruct((zs * block, width), kind), jax.ShapeDtypeStruct((full, width), jnp.float32)]
        out_specs = [pl.BlockSpec((block, width), lambda i, w: (i, 0)), term]
    return pl.pallas_call(
        kernel,
        out_shape=out_shape,
        grid_spec=pltpu.PrefetchScalarGridSpec(
            num_scalar_prefetch=1, grid=(zs,), in_specs=in_specs, out_specs=out_specs
        ),
        compiler_params=pltpu.CompilerParams(vmem_limit_bytes=40 * 2**20),
        cost_estimate=pl.CostEstimate(
            flops=2 * zs * block * cols, bytes_accessed=zs * block * width, transcendentals=0
        ),
    )(place, weight, masked, factor, *extra)


def fetch_factor(own):
    n_row, n_col = lax.axis_size("row"), lax.axis_size("col")
    if n_row == 2:
        return swap_row(own, 1)
    ratio = n_col // n_row
    got = own
    for d in range(1, n_row):
        pairs = [((j // ratio) * n_col + j, ((j // ratio + d) % n_row) * n_col + j) for j in range(n_col)]
        arrived = lax.ppermute(own, ("row", "col"), pairs)
        got = arrived if d == 1 else got + arrived
    return got


def body(inv_block, block_masks, panel_first, panel_second, diag_inverse, weights):
    n_row, n_col, n_pole = (lax.axis_size(a) for a in ("row", "col", "pole"))
    row, col, pole = (lax.axis_index(a) for a in ("row", "col", "pole"))
    zs = n_col // CORES
    z, core = col // CORES, col % CORES
    inverse, weight = inv_block[0], weights[0]
    rows, cols = inverse.shape
    width = panel_first.shape[2]
    wide = width // CHUNKS
    blocks = n_col * n_pole
    block = rows // blocks
    sizes = (zs, block, n_pole)
    panels = (panel_first[0], panel_second[0])
    grain = rows // block_masks.shape[1]
    groups = max(1, block // grain)
    parts = [(k, n) for k in range(2) for n in range(CHUNKS)]

    ratio = n_col // n_row
    mine = row == col // ratio
    own, got = [], []
    for k, n in parts:
        piece = lax.dynamic_slice(panels[k], (col % ratio * cols, n * wide), (cols, wide))
        own.append(piece)
        got.append(fetch_factor(after(piece, *got[-1:])))

    mask = jnp.repeat(block_masks.astype(jnp.bfloat16), grain * groups // block, axis=1)
    mask = jnp.repeat(mask, grain, axis=2).reshape(2, blocks, groups, cols)
    masked = apply_masks(inverse, mask)

    def place(c, d, *deps):
        return after(jnp.stack([c, (pole + d) % n_pole]).astype(jnp.int32), *deps)

    dests = list(range(1, n_pole)) + [0]
    token = (masked[0],)
    units, terms = [], []
    for part, (k, n) in enumerate(parts):
        factor = jnp.where(mine, own[part], after(got[part], *token))
        received, arrived = {}, []
        for d in dests:
            away = product(masked[k], factor, place(1 - core, d, *token), weights, sizes)
            token = (away[0],)
            received[d] = [swap_core(x) for x in away]
        term = jnp.zeros((width, wide), jnp.float32)
        for d in dests if part + 1 < len(parts) else dests[::-1]:
            if d == 0:
                for unit in units:
                    if not unit.done():
                        token += (unit.step(),)
            kind = jnp.bfloat16 if d > 0 else jnp.float32
            out, term = product(
                masked[k], factor, place(core, d, *token), weights, sizes, (received[d], panels[k], term, kind)
            )
            token = (out,)
            if d == 0:
                kept = out
            else:
                arrived.append(lax.ppermute(out, "pole", [(i, (i + d) % n_pole) for i in range(n_pole)]))
        terms.append(term)
        units.append(ZSum([x.reshape(zs, block, wide) for x in [kept] + arrived], z))

    each = width // (n_row * blocks)
    split = (2, n_row, zs, CORES, n_pole, each, width)
    term = jnp.stack([jnp.concatenate(terms[k * CHUNKS:(k + 1) * CHUNKS], axis=1) for k in range(2)]).reshape(split)
    term = halve(term, 3, core, swap_core, jnp.bfloat16)
    term = halve(term, 1, row, swap_row, jnp.bfloat16)
    token = (term,)
    for unit in units[:-1]:
        while not unit.done():
            token += (unit.step(term),)
    first = jnp.concatenate([u.result(*token[1:]) for u in units[:CHUNKS]], axis=1)
    squares = jnp.sum(first * first, axis=0)
    term = halve(after(term, *token[1:]), 1, z, swap_z, jnp.bfloat16)
    base = pick(pick(pick(diag_inverse.reshape(split), core, 3), row, 1), z, 1).astype(jnp.float32) * weight
    both = halve(jnp.stack([base, term]), 2, pole, swap_pole, jnp.float32)
    base, term = both[0], both[1]
    piece = jnp.stack([base[0] + term[0], base[1], term[1]]).astype(jnp.bfloat16)
    piece = piece[:, None, None, None, None]
    for bit in reversed(range(n_pole.bit_length() - 1)):
        piece, squares = double(piece, squares, 4, pole, bit, swap_pole)
    piece = after(piece, units[-1].step(piece))
    for bit in reversed(range(zs.bit_length() - 1)):
        piece, squares = double(piece, squares, 2, z, bit, swap_z)
    while not units[-1].done():
        piece = after(piece, units[-1].step(piece))
    for bit in reversed(range(n_row.bit_length() - 1)):
        piece, squares = double(piece, squares, 1, row, bit, swap_row)
    piece, squares = double(piece, squares, 3, core, 0, swap_core)
    scale = jnp.sqrt(squares / (rows * n_row) + 1e-06)
    piece = piece.reshape(3, width, width).astype(jnp.float32)
    scaled = piece[1] + piece[2] / (scale[:, None] * scale)
    second = jnp.concatenate([u.result() for u in units[CHUNKS:]], axis=1) / scale
    return jnp.stack([first.astype(jnp.bfloat16), second.astype(jnp.bfloat16)]), jnp.stack([piece[0], scaled])


def solution(mesh):
    placed = (
        P("pole", "row", "col"),
        P(None, "row", "col"),
        P("pole", "row", None),
        P("pole", "row", None),
        P(None, "pole", None, None),
        P("pole"),
    )
    return jax.shard_map(
        body,
        mesh=mesh,
        in_specs=placed,
        out_specs=(P(None, ("row", "col", "pole"), None), P()),
        check_vma=False,
    )
```

```python
import jax
import jax.numpy as jnp
from jax import lax
from jax.experimental import pallas as pl
from jax.experimental.pallas import tpu as pltpu
from jax.sharding import PartitionSpec as P

CORES = 2
AWAY = 2
PIECES = (1, 2)


def swap(x, axis, mask):
    size = lax.axis_size(axis)
    return lax.ppermute(x, axis, [(i, i ^ mask) for i in range(size)])


def swap_core(x, mask=1):
    return swap(x, "col", mask)


def swap_z(x, mask):
    return swap(x, "col", mask * CORES)


def swap_row(x, mask):
    return swap(x, "row", mask)


def swap_pole(x, mask):
    return swap(x, "pole", mask)


def after(x, *deps):
    if not deps:
        return x
    return lax.optimization_barrier((x,) + deps)[0]


def pick(x, index, axis):
    return lax.dynamic_index_in_dim(x, index, axis, keepdims=False)


def halve(x, axis, index, exchange, kind):
    bit = 0
    while x.shape[axis] > 1:
        size = x.shape[axis]
        pairs = x.reshape(x.shape[:axis] + (size // 2, 2) + x.shape[axis + 1:])
        low = (index >> bit) & 1
        send = pick(pairs, 1 - low, axis + 1).astype(kind)
        x = pick(pairs, low, axis + 1).astype(jnp.float32) + exchange(send, 1 << bit).astype(jnp.float32)
        bit += 1
    return x.reshape(x.shape[:axis] + x.shape[axis + 1:])


def split_three(x):
    terms = []
    for _ in range(3):
        high = lax.reduce_precision(x, 8, 7)
        terms.append(high.astype(jnp.bfloat16))
        x = x - high
    return jnp.stack(terms)


def double(x, squares, axis, index, bit, exchange):
    count = x.size // x.shape[-1]
    message = jnp.concatenate([x.reshape(count, x.shape[-1]), split_three(squares)])
    other = exchange(message, 1 << bit)
    squares = squares + jnp.sum(other[count:].astype(jnp.float32), axis=0)
    other = other[:count].reshape(x.shape)
    low = (index >> bit) & 1
    both = jnp.where(low == 0, jnp.stack([x, other], axis + 1), jnp.stack([other, x], axis + 1))
    return both.reshape(x.shape[:axis] + (2 * x.shape[axis],) + x.shape[axis + 1:]), squares


class ZSum:
    def __init__(self, sources, z):
        self.sources, self.z, self.bit = [(x, 0) for x in sources], z, 0
        self.bits = sources[0].shape[0].bit_length() - 1

    def part(self, flip, *deps):
        total = 0.0
        for x, depth in self.sources:
            spread = 1 << (self.bit - depth + flip)
            index = (self.z >> depth) & (spread - 1)
            if flip:
                index = index ^ (spread >> 1)
            x = x.reshape((x.shape[0] // spread, spread) + x.shape[1:])
            total = total + pick(after(x, *deps), index, 1).astype(jnp.float32)
        return total

    def step(self, *deps):
        send = self.part(1, *deps).astype(jnp.bfloat16)
        came = swap_z(send, 1 << self.bit)
        self.bit += 1
        self.sources.append((came, self.bit))
        return send

    def done(self):
        return self.bit == self.bits

    def result(self, *deps):
        x = self.part(0, *deps)
        return x.reshape(x.shape[1:])


def weighted_product(a_ref, mask_ref, f_ref, weight_ref):
    rows, cols = a_ref.shape
    groups = mask_ref.shape[1]
    shaped = a_ref[...].reshape(groups, rows // groups, cols)
    masked = (shaped * mask_ref[0][:, None, :]).reshape(rows, cols)
    return jnp.dot(masked, f_ref[...], preferred_element_type=jnp.float32) * weight_ref[0]


def away_kernel(where_ref, weight_ref, a_ref, mask_ref, f_ref, *outs):
    total = weighted_product(a_ref, mask_ref, f_ref, weight_ref)
    width = total.shape[1] // len(outs)
    for n, out_ref in enumerate(outs):
        out_ref[...] = total[:, n * width:(n + 1) * width].astype(out_ref.dtype)


def here_kernel(where_ref, weight_ref, a_ref, mask_ref, f_ref, panel_ref, start_ref, *refs):
    recvs, outs, term_ref = refs[:AWAY], refs[AWAY:-1], refs[-1]
    total = weighted_product(a_ref, mask_ref, f_ref, weight_ref)
    total = total + jnp.concatenate([r[...].astype(jnp.float32) for r in recvs], axis=1)
    width = total.shape[1] // len(outs)
    for n, out_ref in enumerate(outs):
        out_ref[...] = total[:, n * width:(n + 1) * width].astype(out_ref.dtype)
    term = lax.dot_general(
        panel_ref[...], total.astype(jnp.bfloat16), (((0,), (0,)), ((), ())), preferred_element_type=jnp.float32
    )

    @pl.when(pl.program_id(0) == 0)
    def _():
        term_ref[...] = start_ref[...] - term

    @pl.when(pl.program_id(0) > 0)
    def _():
        term_ref[...] = term_ref[...] - term


def product(inverse, mask, factor, place, weight, sizes, merge=None):
    zs, block, n_pole = sizes
    cols = inverse.shape[1]
    width = factor.shape[1]

    def block_of(i, where):
        return (i * CORES + where[0]) * n_pole + where[1]

    in_specs = [
        pl.BlockSpec(memory_space=pltpu.SMEM),
        pl.BlockSpec((block, cols), lambda i, w: (block_of(i, w), 0)),
        pl.BlockSpec((1, mask.shape[1], cols), lambda i, w: (block_of(i, w), 0, 0)),
        pl.BlockSpec((cols, width), lambda i, w: (0, 0)),
    ]
    part = [pl.BlockSpec((block, width // AWAY), lambda i, w: (i, 0))] * AWAY
    if merge is None:
        kernel, extra = away_kernel, ()
        out_shape = [jax.ShapeDtypeStruct((zs * block, width // AWAY), jnp.bfloat16)] * AWAY
        out_specs = part
    else:
        recv, panel, start, kind, pieces = merge
        kernel, extra = here_kernel, (panel, start, *recv)
        full = panel.shape[1]
        term = pl.BlockSpec((full, width), lambda i, w: (0, 0))
        in_specs += [pl.BlockSpec((block, full), lambda i, w: (block_of(i, w), 0)), term] + part
        piece = width // pieces
        out_shape = [jax.ShapeDtypeStruct((zs * block, piece), kind)] * pieces
        out_shape.append(jax.ShapeDtypeStruct((full, width), jnp.float32))
        out_specs = [pl.BlockSpec((block, piece), lambda i, w: (i, 0))] * pieces + [term]
    return pl.pallas_call(
        kernel,
        out_shape=out_shape,
        grid_spec=pltpu.PrefetchScalarGridSpec(
            num_scalar_prefetch=1, grid=(zs,), in_specs=in_specs, out_specs=out_specs
        ),
        compiler_params=pltpu.CompilerParams(vmem_limit_bytes=40 * 2**20),
        cost_estimate=pl.CostEstimate(
            flops=2 * zs * block * cols, bytes_accessed=zs * block * width, transcendentals=0
        ),
    )(place, weight, inverse, mask, factor, *extra)


def fetch_factor(own):
    n_row, n_col = lax.axis_size("row"), lax.axis_size("col")
    if n_row == 2:
        return swap_row(own, 1)
    ratio = n_col // n_row
    got = own
    for d in range(1, n_row):
        pairs = [((j // ratio) * n_col + j, ((j // ratio + d) % n_row) * n_col + j) for j in range(n_col)]
        arrived = lax.ppermute(own, ("row", "col"), pairs)
        got = arrived if d == 1 else got + arrived
    return got


def body(inv_block, block_masks, panel_first, panel_second, diag_inverse, weights):
    n_row, n_col, n_pole = (lax.axis_size(a) for a in ("row", "col", "pole"))
    row, col, pole = (lax.axis_index(a) for a in ("row", "col", "pole"))
    zs = n_col // CORES
    z, core = col // CORES, col % CORES
    inverse, weight = inv_block[0], weights[0]
    rows, cols = inverse.shape
    width = panel_first.shape[2]
    blocks = n_col * n_pole
    block = rows // blocks
    sizes = (zs, block, n_pole)
    panels = (panel_first[0], panel_second[0])
    grain = rows // block_masks.shape[1]
    groups = max(1, block // grain)

    ratio = n_col // n_row
    mine = row == col // ratio
    own, got = [], []
    for panel in panels:
        piece = lax.dynamic_slice(panel, (col % ratio * cols, 0), (cols, width))
        own.append(piece)
        got.append(fetch_factor(after(piece, *got)))

    masks = []
    for k in range(2):
        mask = jnp.repeat(block_masks[k].astype(jnp.bfloat16), grain * groups // block, axis=0)
        masks.append(jnp.repeat(mask, grain, axis=1).reshape(blocks, groups, cols))

    def place(c, d, *deps):
        return after(jnp.stack([c, (pole + d) % n_pole]).astype(jnp.int32), *deps)

    dests = list(range(1, n_pole)) + [0]
    token = tuple(masks)
    units, terms = [], []
    for k in range(2):
        factor = jnp.where(mine, own[k], after(got[k], *token))
        received, arrived = {}, [[] for _ in range(PIECES[k])]
        for d in dests:
            away = product(inverse, masks[k], factor, place(1 - core, d, *token), weights, sizes)
            token = (away[0],)
            received[d] = [swap_core(x) for x in away]
        term = jnp.zeros((width, width), jnp.float32)
        for d in dests:
            if d == 0:
                token += tuple(unit.step() for unit in units)
            kind = jnp.bfloat16 if d > 0 else jnp.float32
            merge = (received[d], panels[k], term, kind, PIECES[k])
            *out, term = product(inverse, masks[k], factor, place(core, d, *token), weights, sizes, merge)
            token = (out[0],)
            if d > 0:
                before = ()
                for n, x in enumerate(out):
                    came = lax.ppermute(after(x, *before), "pole", [(i, (i + d) % n_pole) for i in range(n_pole)])
                    before = (came,)
                    arrived[n].append(came)
        terms.append(term)
        for n, kept in enumerate(out):
            units.append(ZSum([x.reshape(zs, block, x.shape[1]) for x in [kept] + arrived[n]], z))

    zero, early, last = units
    each = width // (n_row * blocks)
    split = (2, n_row, zs, CORES, n_pole, each, width)
    term = halve(jnp.stack(terms).reshape(split), 3, core, swap_core, jnp.bfloat16)
    term = after(term, early.step(*token))
    term = halve(term, 1, row, swap_row, jnp.bfloat16)
    while not zero.done():
        term = after(term, zero.step())
    term = halve(term, 1, z, swap_z, jnp.bfloat16)
    while not early.done():
        term = after(term, early.step(term))
    first = zero.result(term)
    squares = jnp.sum(first * first, axis=0)
    term = after(term, squares, last.step(term))
    base = pick(pick(pick(diag_inverse.reshape(split), core, 3), row, 1), z, 1).astype(jnp.float32) * weight
    both = halve(jnp.stack([base, term]), 2, pole, swap_pole, jnp.float32)
    base, term = both[0], both[1]
    piece = jnp.stack([base[0] + term[0], base[1], term[1]]).astype(jnp.bfloat16)
    piece = piece[:, None, None, None, None]
    for bit in reversed(range(n_pole.bit_length() - 1)):
        piece, squares = double(piece, squares, 4, pole, bit, swap_pole)
    while not last.done():
        piece = after(piece, last.step(piece))
    for bit in reversed(range(zs.bit_length() - 1)):
        piece, squares = double(piece, squares, 2, z, bit, swap_z)
    for bit in reversed(range(n_row.bit_length() - 1)):
        piece, squares = double(piece, squares, 1, row, bit, swap_row)
    second = jnp.concatenate([early.result(), last.result()], axis=1)
    piece = after(piece, second)
    piece, squares = double(piece, squares, 3, core, 0, swap_core)
    scale = jnp.sqrt(squares / (rows * n_row) + 1e-06)
    piece = piece.reshape(3, width, width).astype(jnp.float32)
    scaled = piece[1] + piece[2] / (scale[:, None] * scale)
    second = second / scale
    return jnp.stack([first.astype(jnp.bfloat16), second.astype(jnp.bfloat16)]), jnp.stack([piece[0], scaled])


def solution(mesh):
    placed = (
        P("pole", "row", "col"),
        P(None, "row", "col"),
        P("pole", "row", None),
        P("pole", "row", None),
        P(None, "pole", None, None),
        P("pole"),
    )
    return jax.shard_map(
        body,
        mesh=mesh,
        in_specs=placed,
        out_specs=(P(None, ("row", "col", "pole"), None), P()),
        check_vma=False,
    )
```

```python
import jax
import jax.numpy as jnp
from jax import lax
from jax.experimental import pallas as pl
from jax.experimental.pallas import tpu as pltpu
from jax.sharding import PartitionSpec as P

CORES = 2
AWAY = 2
PIECES = (1, 2)


def swap(x, axis, mask):
    size = lax.axis_size(axis)
    return lax.ppermute(x, axis, [(i, i ^ mask) for i in range(size)])


def swap_core(x, mask=1):
    return swap(x, "col", mask)


def swap_z(x, mask):
    return swap(x, "col", mask * CORES)


def swap_row(x, mask):
    return swap(x, "row", mask)


def swap_pole(x, mask):
    return swap(x, "pole", mask)


def after(x, *deps):
    if not deps:
        return x
    return lax.optimization_barrier((x,) + deps)[0]


def pick(x, index, axis):
    return lax.dynamic_index_in_dim(x, index, axis, keepdims=False)


def halve(x, axis, index, exchange, kind):
    bit = 0
    while x.shape[axis] > 1:
        size = x.shape[axis]
        pairs = x.reshape(x.shape[:axis] + (size // 2, 2) + x.shape[axis + 1:])
        low = (index >> bit) & 1
        send = pick(pairs, 1 - low, axis + 1).astype(kind)
        x = pick(pairs, low, axis + 1).astype(jnp.float32) + exchange(send, 1 << bit).astype(jnp.float32)
        bit += 1
    return x.reshape(x.shape[:axis] + x.shape[axis + 1:])


def split_three(x):
    terms = []
    for _ in range(3):
        high = lax.reduce_precision(x, 8, 7)
        terms.append(high.astype(jnp.bfloat16))
        x = x - high
    return jnp.stack(terms)


def double(x, squares, axis, index, bit, exchange):
    count = x.size // x.shape[-1]
    message = jnp.concatenate([x.reshape(count, x.shape[-1]), split_three(squares)])
    other = exchange(message, 1 << bit)
    squares = squares + jnp.sum(other[count:].astype(jnp.float32), axis=0)
    other = other[:count].reshape(x.shape)
    low = (index >> bit) & 1
    both = jnp.where(low == 0, jnp.stack([x, other], axis + 1), jnp.stack([other, x], axis + 1))
    return both.reshape(x.shape[:axis] + (2 * x.shape[axis],) + x.shape[axis + 1:]), squares


class ZSum:
    def __init__(self, sources, z):
        self.sources, self.z, self.bit = [(x, 0) for x in sources], z, 0
        self.bits = sources[0].shape[0].bit_length() - 1

    def part(self, flip, *deps):
        total = 0.0
        for x, depth in self.sources:
            spread = 1 << (self.bit - depth + flip)
            index = (self.z >> depth) & (spread - 1)
            if flip:
                index = index ^ (spread >> 1)
            x = x.reshape((x.shape[0] // spread, spread) + x.shape[1:])
            total = total + pick(after(x, *deps), index, 1).astype(jnp.float32)
        return total

    def step(self, *deps):
        send = self.part(1, *deps).astype(jnp.bfloat16)
        came = swap_z(send, 1 << self.bit)
        self.bit += 1
        self.sources.append((came, self.bit))
        return send

    def done(self):
        return self.bit == self.bits

    def result(self, *deps):
        x = self.part(0, *deps)
        return x.reshape(x.shape[1:])


def weighted_product(a_ref, mask_ref, f_ref, weight_ref):
    rows, cols = a_ref.shape
    groups = mask_ref.shape[1]
    shaped = a_ref[...].reshape(groups, rows // groups, cols)
    masked = (shaped * mask_ref[0][:, None, :]).reshape(rows, cols)
    return jnp.dot(masked, f_ref[...], preferred_element_type=jnp.float32) * weight_ref[0]


def away_kernel(where_ref, weight_ref, a_ref, mask_ref, f_ref, *outs):
    total = weighted_product(a_ref, mask_ref, f_ref, weight_ref)
    width = total.shape[1] // len(outs)
    for n, out_ref in enumerate(outs):
        out_ref[...] = total[:, n * width:(n + 1) * width].astype(out_ref.dtype)


def here_kernel(where_ref, weight_ref, a_ref, mask_ref, f_ref, panel_ref, start_ref, *refs):
    recvs, outs, term_ref = refs[:AWAY], refs[AWAY:-1], refs[-1]
    total = weighted_product(a_ref, mask_ref, f_ref, weight_ref)
    total = total + jnp.concatenate([r[...].astype(jnp.float32) for r in recvs], axis=1)
    width = total.shape[1] // len(outs)
    for n, out_ref in enumerate(outs):
        out_ref[...] = total[:, n * width:(n + 1) * width].astype(out_ref.dtype)
    term = lax.dot_general(
        panel_ref[...], total.astype(jnp.bfloat16), (((0,), (0,)), ((), ())), preferred_element_type=jnp.float32
    )

    @pl.when(pl.program_id(0) == 0)
    def _():
        term_ref[...] = start_ref[...] - term

    @pl.when(pl.program_id(0) > 0)
    def _():
        term_ref[...] = term_ref[...] - term


def product(inverse, mask, factor, place, weight, sizes, merge=None):
    zs, block, n_pole = sizes
    cols = inverse.shape[1]
    width = factor.shape[1]

    def block_of(i, where):
        return (i * CORES + where[0]) * n_pole + where[1]

    in_specs = [
        pl.BlockSpec(memory_space=pltpu.SMEM),
        pl.BlockSpec((block, cols), lambda i, w: (block_of(i, w), 0)),
        pl.BlockSpec((1, mask.shape[1], cols), lambda i, w: (block_of(i, w), 0, 0)),
        pl.BlockSpec((cols, width), lambda i, w: (0, 0)),
    ]
    part = [pl.BlockSpec((block, width // AWAY), lambda i, w: (i, 0))] * AWAY
    if merge is None:
        kernel, extra = away_kernel, ()
        out_shape = [jax.ShapeDtypeStruct((zs * block, width // AWAY), jnp.bfloat16)] * AWAY
        out_specs = part
    else:
        recv, panel, start, kind, pieces = merge
        kernel, extra = here_kernel, (panel, start, *recv)
        full = panel.shape[1]
        term = pl.BlockSpec((full, width), lambda i, w: (0, 0))
        in_specs += [pl.BlockSpec((block, full), lambda i, w: (block_of(i, w), 0)), term] + part
        piece = width // pieces
        out_shape = [jax.ShapeDtypeStruct((zs * block, piece), kind)] * pieces
        out_shape.append(jax.ShapeDtypeStruct((full, width), jnp.float32))
        out_specs = [pl.BlockSpec((block, piece), lambda i, w: (i, 0))] * pieces + [term]
    return pl.pallas_call(
        kernel,
        out_shape=out_shape,
        grid_spec=pltpu.PrefetchScalarGridSpec(
            num_scalar_prefetch=1, grid=(zs,), in_specs=in_specs, out_specs=out_specs
        ),
        compiler_params=pltpu.CompilerParams(vmem_limit_bytes=40 * 2**20),
        cost_estimate=pl.CostEstimate(
            flops=2 * zs * block * cols, bytes_accessed=zs * block * width, transcendentals=0
        ),
    )(place, weight, inverse, mask, factor, *extra)


def fetch_factor(panel, cols, row, col, *deps):
    n_row, n_col = lax.axis_size("row"), lax.axis_size("col")
    zs, ratio, width = n_col // CORES, n_col // n_row, panel.shape[1]

    def mirror(j):
        return (zs - 1 - j // CORES) * CORES + j % CORES

    def cross(x, place):
        got = None
        for d in range(1, n_row):
            pairs = []
            for j in range(n_col):
                owner = j // ratio
                pairs.append((owner * n_col + place(j), (owner + d) % n_row * n_col + place(j)))
            arrived = lax.ppermute(x, ("row", "col"), pairs)
            got = arrived if got is None else got + arrived
        return x if got is None else got

    far = cols // 4 if n_row == 2 and zs > 1 else 0
    own = lax.dynamic_slice(panel, (col % ratio * cols, 0), (cols, width))
    got = [cross(after(own[:cols - far], *deps), lambda j: j)]
    if far > 0:
        other = lax.dynamic_slice(panel, (mirror(col) % ratio * cols + cols - far, 0), (far, width))
        crossed = cross(after(other, *deps), mirror)
        got.append(lax.ppermute(crossed, "col", [(j, mirror(j)) for j in range(n_col)]))
    return own, got


def body(inv_block, block_masks, panel_first, panel_second, diag_inverse, weights):
    n_row, n_col, n_pole = (lax.axis_size(a) for a in ("row", "col", "pole"))
    row, col, pole = (lax.axis_index(a) for a in ("row", "col", "pole"))
    zs = n_col // CORES
    z, core = col // CORES, col % CORES
    inverse, weight = inv_block[0], weights[0]
    rows, cols = inverse.shape
    width = panel_first.shape[2]
    blocks = n_col * n_pole
    block = rows // blocks
    sizes = (zs, block, n_pole)
    panels = (panel_first[0], panel_second[0])
    grain = rows // block_masks.shape[1]
    groups = max(1, block // grain)

    ratio = n_col // n_row
    mine = row == col // ratio
    own, got = [], []
    for panel in panels:
        mine_rows, others = fetch_factor(panel, cols, row, col, *(got[-1] if got else ()))
        own.append(mine_rows)
        got.append(others)

    masks = []
    for k in range(2):
        mask = jnp.repeat(block_masks[k].astype(jnp.bfloat16), grain * groups // block, axis=0)
        masks.append(jnp.repeat(mask, grain, axis=1).reshape(blocks, groups, cols))

    def place(c, d, *deps):
        return after(jnp.stack([c, (pole + d) % n_pole]).astype(jnp.int32), *deps)

    dests = list(range(1, n_pole)) + [0]
    token = tuple(masks)
    units, terms = [], []
    for k in range(2):
        factor = jnp.where(mine, own[k], after(jnp.concatenate(got[k]), *token))
        received, arrived = {}, [[] for _ in range(PIECES[k])]
        for d in dests:
            away = product(inverse, masks[k], factor, place(1 - core, d, *token), weights, sizes)
            token = (away[0],)
            received[d] = [swap_core(x) for x in away]
        term = jnp.zeros((width, width), jnp.float32)
        for d in dests:
            if d == 0:
                token += tuple(unit.step() for unit in units)
            kind = jnp.bfloat16 if d > 0 else jnp.float32
            merge = (received[d], panels[k], term, kind, PIECES[k])
            *out, term = product(inverse, masks[k], factor, place(core, d, *token), weights, sizes, merge)
            token = (out[0],)
            if d > 0:
                before = ()
                for n, x in enumerate(out):
                    came = lax.ppermute(after(x, *before), "pole", [(i, (i + d) % n_pole) for i in range(n_pole)])
                    before = (came,)
                    arrived[n].append(came)
        terms.append(term)
        for n, kept in enumerate(out):
            units.append(ZSum([x.reshape(zs, block, x.shape[1]) for x in [kept] + arrived[n]], z))

    zero, early, last = units
    each = width // (n_row * blocks)
    split = (2, n_row, zs, CORES, n_pole, each, width)
    term = halve(jnp.stack(terms).reshape(split), 3, core, swap_core, jnp.bfloat16)
    term = after(term, early.step(*token))
    if not zero.done():
        term = after(term, zero.step())
    term = halve(term, 1, row, swap_row, jnp.bfloat16)
    term = after(term, last.step(term))
    term = halve(term, 1, z, swap_z, jnp.bfloat16)
    while not zero.done():
        term = after(term, zero.step(term))
    while not early.done():
        term = after(term, early.step(term))
    first = zero.result(term)
    squares = jnp.sum(first * first, axis=0)
    base = pick(pick(pick(diag_inverse.reshape(split), core, 3), row, 1), z, 1).astype(jnp.float32) * weight
    both = halve(jnp.stack([base, after(term, squares)]), 2, pole, swap_pole, jnp.float32)
    base, term = both[0], both[1]
    piece = jnp.stack([base[0] + term[0], base[1], term[1]]).astype(jnp.bfloat16)
    piece = piece[:, None, None, None, None]
    for bit in reversed(range(n_pole.bit_length() - 1)):
        piece, squares = double(piece, squares, 4, pole, bit, swap_pole)
    while not last.done():
        piece = after(piece, last.step(piece))
    piece, second = lax.optimization_barrier((piece, early.result(piece)))
    for bit in reversed(range(zs.bit_length() - 1)):
        piece, squares = double(piece, squares, 2, z, bit, swap_z)
    piece, *second = lax.optimization_barrier((piece, second, last.result(piece)))
    for bit in reversed(range(n_row.bit_length() - 1)):
        piece, squares = double(piece, squares, 1, row, bit, swap_row)
    piece, squares = double(piece, squares, 3, core, 0, swap_core)
    scale = jnp.sqrt(squares / (rows * n_row) + 1e-06)
    piece = piece.reshape(3, width, width).astype(jnp.float32)
    scaled = piece[1] + piece[2] / (scale[:, None] * scale)
    second = jnp.concatenate(second, axis=1) / scale
    return jnp.stack([first.astype(jnp.bfloat16), second.astype(jnp.bfloat16)]), jnp.stack([piece[0], scaled])


def solution(mesh):
    placed = (
        P("pole", "row", "col"),
        P(None, "row", "col"),
        P("pole", "row", None),
        P("pole", "row", None),
        P(None, "pole", None, None),
        P("pole"),
    )
    return jax.shard_map(
        body,
        mesh=mesh,
        in_specs=placed,
        out_specs=(P(None, ("row", "col", "pole"), None), P()),
        check_vma=False,
    )
```

```python
import functools

import jax
import jax.numpy as jnp
from jax import lax
from jax.experimental import pallas as pl
from jax.experimental.pallas import tpu as pltpu
from jax.sharding import PartitionSpec as P

CORES = 2
SLICES = 4
PARTS = ((0, 0, 1, 1), (0, 1, 1, 1), (1, 0, 2, 2))


def swap(x, axis, mask):
    size = lax.axis_size(axis)
    return lax.ppermute(x, axis, [(i, i ^ mask) for i in range(size)])


def swap_core(x, mask=1):
    return swap(x, "col", mask)


def swap_z(x, mask):
    return swap(x, "col", mask * CORES)


def swap_row(x, mask):
    return swap(x, "row", mask)


def swap_pole(x, mask):
    return swap(x, "pole", mask)


def after(x, *deps):
    if not deps:
        return x
    return lax.optimization_barrier((x,) + deps)[0]


def pick(x, index, axis):
    return lax.dynamic_index_in_dim(x, index, axis, keepdims=False)


def halve(x, axis, index, exchange, kind, before_last=None):
    bit = 0
    while x.shape[axis] > 1:
        size = x.shape[axis]
        if size == 2 and before_last is not None:
            x = after(x, before_last())
        pairs = x.reshape(x.shape[:axis] + (size // 2, 2) + x.shape[axis + 1:])
        low = (index >> bit) & 1
        send = pick(pairs, 1 - low, axis + 1).astype(kind)
        x = pick(pairs, low, axis + 1).astype(jnp.float32) + exchange(send, 1 << bit).astype(jnp.float32)
        bit += 1
    return x.reshape(x.shape[:axis] + x.shape[axis + 1:])


def split_three(x):
    terms = []
    for _ in range(3):
        high = lax.reduce_precision(x, 8, 7)
        terms.append(high.astype(jnp.bfloat16))
        x = x - high
    return jnp.stack(terms)


def double(x, squares, axis, index, bit, exchange):
    count = x.size // x.shape[-1]
    message = jnp.concatenate([x.reshape(count, x.shape[-1]), split_three(squares)])
    other = exchange(message, 1 << bit)
    squares = squares + jnp.sum(other[count:].astype(jnp.float32), axis=0)
    other = other[:count].reshape(x.shape)
    low = (index >> bit) & 1
    both = jnp.where(low == 0, jnp.stack([x, other], axis + 1), jnp.stack([other, x], axis + 1))
    return both.reshape(x.shape[:axis] + (2 * x.shape[axis],) + x.shape[axis + 1:]), squares


class ZSum:
    def __init__(self, sources, z):
        self.sources, self.z, self.bit = [(x, 0) for x in sources], z, 0
        self.bits = sources[0].shape[0].bit_length() - 1
        self.total = None

    def part(self, flip, *deps):
        total = 0.0
        for x, depth in self.sources:
            spread = 1 << (self.bit - depth + flip)
            index = (self.z >> depth) & (spread - 1)
            if flip:
                index = index ^ (spread >> 1)
            x = x.reshape((x.shape[0] // spread, spread) + x.shape[1:])
            total = total + pick(after(x, *deps), index, 1).astype(jnp.float32)
        return total

    def step(self, *deps):
        send = self.part(1, *deps).astype(jnp.bfloat16)
        came = swap_z(send, 1 << self.bit)
        self.bit += 1
        self.sources.append((came, self.bit))
        return send

    def done(self):
        return self.bit == self.bits

    def result(self, *deps):
        if self.total is not None:
            return self.total
        x = self.part(0, *deps)
        return x.reshape(x.shape[1:])


def weighted_product(a_ref, mask_ref, f_ref, weight_ref):
    rows, cols = a_ref.shape
    groups = mask_ref.shape[1]
    shaped = a_ref[...].reshape(groups, rows // groups, cols)
    masked = (shaped * mask_ref[0][:, None, :]).reshape(rows, cols)
    return jnp.dot(masked, f_ref[...], preferred_element_type=jnp.float32) * weight_ref[0]


def away_kernel(where_ref, weight_ref, a_ref, mask_ref, f_ref, *outs):
    total = weighted_product(a_ref, mask_ref, f_ref, weight_ref)
    width = total.shape[1] // len(outs)
    for n, out_ref in enumerate(outs):
        out_ref[...] = total[:, n * width:(n + 1) * width].astype(out_ref.dtype)


def here_kernel(slices, where_ref, weight_ref, a_ref, mask_ref, f_ref, panel_ref, start_ref, *refs):
    recvs, outs, term_ref = refs[:slices], refs[slices:-1], refs[-1]
    total = weighted_product(a_ref, mask_ref, f_ref, weight_ref)
    total = total + jnp.concatenate([r[...].astype(jnp.float32) for r in recvs], axis=1)
    width = total.shape[1] // len(outs)
    for n, out_ref in enumerate(outs):
        out_ref[...] = total[:, n * width:(n + 1) * width].astype(out_ref.dtype)
    term = lax.dot_general(
        panel_ref[...], total.astype(jnp.bfloat16), (((0,), (0,)), ((), ())), preferred_element_type=jnp.float32
    )

    @pl.when(pl.program_id(0) == 0)
    def _():
        term_ref[...] = start_ref[...] - term

    @pl.when(pl.program_id(0) > 0)
    def _():
        term_ref[...] = term_ref[...] - term


def product(inverse, mask, factor, place, weight, sizes, merge=None):
    zs, block, n_pole, thin = sizes
    cols = inverse.shape[1]
    width = factor.shape[1]

    def block_of(i, where):
        return (i * CORES + where[0]) * n_pole + where[1]

    in_specs = [
        pl.BlockSpec(memory_space=pltpu.SMEM),
        pl.BlockSpec((block, cols), lambda i, w: (block_of(i, w), 0)),
        pl.BlockSpec((1, mask.shape[1], cols), lambda i, w: (block_of(i, w), 0, 0)),
        pl.BlockSpec((cols, width), lambda i, w: (0, 0)),
    ]
    slices = width // thin
    part = [pl.BlockSpec((block, thin), lambda i, w: (i, 0))] * slices
    if merge is None:
        kernel, extra = away_kernel, ()
        out_shape = [jax.ShapeDtypeStruct((zs * block, thin), jnp.bfloat16)] * slices
        out_specs = part
    else:
        recv, panel, start, kind, pieces = merge
        kernel, extra = functools.partial(here_kernel, slices), (panel, start, *recv)
        full = panel.shape[1]
        term = pl.BlockSpec((full, width), lambda i, w: (0, 0))
        in_specs += [pl.BlockSpec((block, full), lambda i, w: (block_of(i, w), 0)), term] + part
        piece = width // pieces
        out_shape = [jax.ShapeDtypeStruct((zs * block, piece), kind)] * pieces
        out_shape.append(jax.ShapeDtypeStruct((full, width), jnp.float32))
        out_specs = [pl.BlockSpec((block, piece), lambda i, w: (i, 0))] * pieces + [term]
    return pl.pallas_call(
        kernel,
        out_shape=out_shape,
        grid_spec=pltpu.PrefetchScalarGridSpec(
            num_scalar_prefetch=1, grid=(zs,), in_specs=in_specs, out_specs=out_specs
        ),
        compiler_params=pltpu.CompilerParams(vmem_limit_bytes=40 * 2**20),
        cost_estimate=pl.CostEstimate(
            flops=2 * zs * block * cols, bytes_accessed=zs * block * width, transcendentals=0
        ),
    )(place, weight, inverse, mask, factor, *extra)


def fetch_factor(panel, cols, columns, detour, row, col, *deps):
    n_row, n_col = lax.axis_size("row"), lax.axis_size("col")
    zs, ratio = n_col // CORES, n_col // n_row
    first, width = columns

    def mirror(j):
        return (zs - 1 - j // CORES) * CORES + j % CORES

    def cross(x, place):
        got = None
        for d in range(1, n_row):
            pairs = []
            for j in range(n_col):
                owner = j // ratio
                pairs.append((owner * n_col + place(j), (owner + d) % n_row * n_col + place(j)))
            arrived = lax.ppermute(x, ("row", "col"), pairs)
            got = arrived if got is None else got + arrived
        return x if got is None else got

    far = cols // 4 if detour and n_row == 2 and zs > 1 else 0
    own = lax.dynamic_slice(panel, (col % ratio * cols, first), (cols, width))
    got = [cross(after(own[:cols - far], *deps), lambda j: j)]
    if far > 0:
        other = lax.dynamic_slice(panel, (mirror(col) % ratio * cols + cols - far, first), (far, width))
        crossed = cross(after(other, *deps), mirror)
        got.append(lax.ppermute(crossed, "col", [(j, mirror(j)) for j in range(n_col)]))
    return own, got


def body(inv_block, block_masks, panel_first, panel_second, diag_inverse, weights):
    n_row, n_col, n_pole = (lax.axis_size(a) for a in ("row", "col", "pole"))
    row, col, pole = (lax.axis_index(a) for a in ("row", "col", "pole"))
    zs = n_col // CORES
    z, core = col // CORES, col % CORES
    inverse, weight = inv_block[0], weights[0]
    rows, cols = inverse.shape
    width = panel_first.shape[2]
    blocks = n_col * n_pole
    block = rows // blocks
    sizes = (zs, block, n_pole, width // SLICES)
    panels = (panel_first[0], panel_second[0])
    grain = rows // block_masks.shape[1]
    groups = max(1, block // grain)

    ratio = n_col // n_row
    mine = row == col // ratio
    half = width // 2
    own, got = [], []
    for k, first, size, _ in PARTS:
        columns = (first * half, size * half)
        mine_rows, others = fetch_factor(panels[k], cols, columns, k == 0, row, col, *(got[-1] if got else ()))
        own.append(mine_rows)
        got.append(others)

    masks = []
    for k in range(2):
        mask = jnp.repeat(block_masks[k].astype(jnp.bfloat16), grain * groups // block, axis=0)
        masks.append(jnp.repeat(mask, grain, axis=1).reshape(blocks, groups, cols))

    def place(c, d, *deps):
        return after(jnp.stack([c, (pole + d) % n_pole]).astype(jnp.int32), *deps)

    dests = list(range(1, n_pole)) + [0]
    token = tuple(masks)
    units, terms = [], [[], []]
    for part, (k, first, size, pieces) in enumerate(PARTS):
        wide = size * half
        factor, start = [], 0
        for x in got[part]:
            x = after(x, *token)
            factor.append(jnp.where(mine, own[part][start:start + x.shape[0]], x))
            start += x.shape[0]
        factor = jnp.concatenate(factor)
        received, arrived = {}, [[] for _ in range(pieces)]
        for d in dests:
            if d == 0:
                token += tuple(unit.step() for unit in units[:-1] if not unit.done())
            away = product(inverse, masks[k], factor, place(1 - core, d, *token), weights, sizes)
            token = (away[0],)
            received[d] = [swap_core(x) for x in away]
        term = jnp.zeros((width, wide), jnp.float32)
        for d in dests:
            if d == 0:
                done = [unit for unit in units if unit.done()]
                token += tuple(unit.step() for unit in units if not unit.done())
                for unit in done:
                    unit.total, *token = lax.optimization_barrier((unit.result(), *token))
            kind = jnp.bfloat16 if d > 0 else jnp.float32
            merge = (received[d], panels[k], term, kind, pieces)
            *out, term = product(inverse, masks[k], factor, place(core, d, *token), weights, sizes, merge)
            token = (out[0],)
            if d > 0:
                before = ()
                for n, x in enumerate(out):
                    came = lax.ppermute(after(x, *before), "pole", [(i, (i + d) % n_pole) for i in range(n_pole)])
                    before = (came,)
                    arrived[n].append(came)
        terms[k].append(term)
        for n, kept in enumerate(out):
            units.append(ZSum([x.reshape(zs, block, x.shape[1]) for x in [kept] + arrived[n]], z))

    *zeros, early, last = units
    each = width // (n_row * blocks)
    split = (2, n_row, zs, CORES, n_pole, each, width)
    term = jnp.stack([jnp.concatenate(t, axis=1) for t in terms]).reshape(split)
    term = halve(term, 3, core, swap_core, jnp.bfloat16)
    term = after(term, early.step(*token))
    for unit in zeros:
        while not unit.done():
            term = after(term, unit.step())
    term = halve(term, 1, row, swap_row, jnp.bfloat16)
    term = halve(term, 1, z, swap_z, jnp.bfloat16, last.step)
    while not early.done():
        term = after(term, early.step(term))
    base = pick(pick(pick(diag_inverse.reshape(split), core, 3), row, 1), z, 1).astype(jnp.float32) * weight
    both = halve(jnp.stack([base, term]), 2, pole, swap_pole, jnp.float32)
    base, term = both[0], both[1]
    piece = jnp.stack([base[0] + term[0], base[1], term[1]]).astype(jnp.bfloat16)
    piece = piece[:, None, None, None, None]
    piece, *firsts = lax.optimization_barrier((piece, *[unit.result() for unit in zeros]))
    first = jnp.concatenate(firsts, axis=1)
    squares = jnp.sum(first * first, axis=0)
    for bit in reversed(range(n_pole.bit_length() - 1)):
        piece, squares = double(piece, squares, 4, pole, bit, swap_pole)
    for bit in reversed(range(zs.bit_length() - 1)):
        piece, squares = double(piece, squares, 2, z, bit, swap_z)
        if not last.done():
            piece = after(piece, last.step(piece))
    piece, second = lax.optimization_barrier((piece, early.result(piece)))
    for bit in reversed(range(n_row.bit_length() - 1)):
        piece, squares = double(piece, squares, 1, row, bit, swap_row)
    while not last.done():
        piece = after(piece, last.step(piece))
    piece, *second = lax.optimization_barrier((piece, second, last.result(piece)))
    piece, squares = double(piece, squares, 3, core, 0, swap_core)
    scale = jnp.sqrt(squares / (rows * n_row) + 1e-06)
    piece = piece.reshape(3, width, width).astype(jnp.float32)
    scaled = piece[1] + piece[2] / (scale[:, None] * scale)
    second = jnp.concatenate(second, axis=1) / scale
    return jnp.stack([first.astype(jnp.bfloat16), second.astype(jnp.bfloat16)]), jnp.stack([piece[0], scaled])


def solution(mesh):
    placed = (
        P("pole", "row", "col"),
        P(None, "row", "col"),
        P("pole", "row", None),
        P("pole", "row", None),
        P(None, "pole", None, None),
        P("pole"),
    )
    return jax.shard_map(
        body,
        mesh=mesh,
        in_specs=placed,
        out_specs=(P(None, ("row", "col", "pole"), None), P()),
        check_vma=False,
    )
```

```python
import functools

import jax
import jax.numpy as jnp
from jax import lax
from jax.experimental import pallas as pl
from jax.experimental.pallas import tpu as pltpu
from jax.sharding import PartitionSpec as P

CORES = 2
SLICES = 4
PARTS = ((0, 0, 1, 1), (0, 1, 1, 1), (1, 0, 2, 2))


def swap(x, axis, mask):
    size = lax.axis_size(axis)
    return lax.ppermute(x, axis, [(i, i ^ mask) for i in range(size)])


def swap_core(x, mask=1):
    return swap(x, "col", mask)


def swap_z(x, mask):
    return swap(x, "col", mask * CORES)


def swap_row(x, mask):
    return swap(x, "row", mask)


def swap_pole(x, mask):
    return swap(x, "pole", mask)


def after(x, *deps):
    if not deps:
        return x
    return lax.optimization_barrier((x,) + deps)[0]


def pick(x, index, axis):
    return lax.dynamic_index_in_dim(x, index, axis, keepdims=False)


def halve(x, axis, index, exchange, kind):
    bit = 0
    while x.shape[axis] > 1:
        size = x.shape[axis]
        pairs = x.reshape(x.shape[:axis] + (size // 2, 2) + x.shape[axis + 1:])
        low = (index >> bit) & 1
        send = pick(pairs, 1 - low, axis + 1).astype(kind)
        x = pick(pairs, low, axis + 1).astype(jnp.float32) + exchange(send, 1 << bit).astype(jnp.float32)
        bit += 1
    return x.reshape(x.shape[:axis] + x.shape[axis + 1:])


def split_three(x):
    terms = []
    for _ in range(3):
        high = lax.reduce_precision(x, 8, 7)
        terms.append(high.astype(jnp.bfloat16))
        x = x - high
    return jnp.stack(terms)


def with_squares(x, squares, exchange, mask):
    count = x.size // x.shape[-1]
    message = jnp.concatenate([x.reshape(count, x.shape[-1]), split_three(squares)])
    other = exchange(message, mask)
    return other[:count].reshape(x.shape), squares + jnp.sum(other[count:].astype(jnp.float32), axis=0)


def add_both(x, squares, exchange, mask, exact=False):
    if exact:
        count = x.size // x.shape[-1]
        message = jnp.concatenate([x.reshape(count, x.shape[-1]), squares[None]])
        message = message + exchange(message, mask)
        return message[:count].reshape(x.shape), message[count]
    x = lax.reduce_precision(x, 8, 7)
    other, squares = with_squares(x.astype(jnp.bfloat16), squares, exchange, mask)
    return x + other.astype(jnp.float32), squares


def double(x, squares, axis, index, bit, exchange):
    other, squares = with_squares(x, squares, exchange, 1 << bit)
    low = (index >> bit) & 1
    both = jnp.where(low == 0, jnp.stack([x, other], axis + 1), jnp.stack([other, x], axis + 1))
    return both.reshape(x.shape[:axis] + (2 * x.shape[axis],) + x.shape[axis + 1:]), squares


class ZSum:
    def __init__(self, sources, z):
        self.sources, self.z, self.bit = [(x, 0) for x in sources], z, 0
        self.bits = sources[0].shape[0].bit_length() - 1
        self.total = None

    def part(self, flip, *deps):
        total = 0.0
        for x, depth in self.sources:
            spread = 1 << (self.bit - depth + flip)
            index = (self.z >> depth) & (spread - 1)
            if flip:
                index = index ^ (spread >> 1)
            x = x.reshape((x.shape[0] // spread, spread) + x.shape[1:])
            total = total + pick(after(x, *deps), index, 1).astype(jnp.float32)
        return total

    def step(self, *deps):
        send = self.part(1, *deps).astype(jnp.bfloat16)
        came = swap_z(send, 1 << self.bit)
        self.bit += 1
        self.sources.append((came, self.bit))
        return send

    def done(self):
        return self.bit == self.bits

    def result(self, *deps):
        if self.total is not None:
            return self.total
        x = self.part(0, *deps)
        return x.reshape(x.shape[1:])


def weighted_product(a_ref, mask_ref, f_ref, weight_ref):
    rows, cols = a_ref.shape
    groups = mask_ref.shape[1]
    shaped = a_ref[...].reshape(groups, rows // groups, cols)
    masked = (shaped * mask_ref[0][:, None, :]).reshape(rows, cols)
    return jnp.dot(masked, f_ref[...], preferred_element_type=jnp.float32) * weight_ref[0]


def away_kernel(where_ref, weight_ref, a_ref, mask_ref, f_ref, *outs):
    total = weighted_product(a_ref, mask_ref, f_ref, weight_ref)
    width = total.shape[1] // len(outs)
    for n, out_ref in enumerate(outs):
        out_ref[...] = total[:, n * width:(n + 1) * width].astype(out_ref.dtype)


def here_kernel(slices, where_ref, weight_ref, a_ref, mask_ref, f_ref, panel_ref, start_ref, *refs):
    recvs, outs, term_ref = refs[:slices], refs[slices:-1], refs[-1]
    total = weighted_product(a_ref, mask_ref, f_ref, weight_ref)
    total = total + jnp.concatenate([r[...].astype(jnp.float32) for r in recvs], axis=1)
    width = total.shape[1] // len(outs)
    for n, out_ref in enumerate(outs):
        out_ref[...] = total[:, n * width:(n + 1) * width].astype(out_ref.dtype)
    term = lax.dot_general(
        panel_ref[...], total.astype(jnp.bfloat16), (((0,), (0,)), ((), ())), preferred_element_type=jnp.float32
    )

    @pl.when(pl.program_id(0) == 0)
    def _():
        term_ref[...] = start_ref[...] - term

    @pl.when(pl.program_id(0) > 0)
    def _():
        term_ref[...] = term_ref[...] - term


def product(inverse, mask, factor, place, weight, sizes, merge=None):
    zs, block, n_pole, thin = sizes
    cols = inverse.shape[1]
    width = factor.shape[1]

    def block_of(i, where):
        return (i * CORES + where[0]) * n_pole + where[1]

    in_specs = [
        pl.BlockSpec(memory_space=pltpu.SMEM),
        pl.BlockSpec((block, cols), lambda i, w: (block_of(i, w), 0)),
        pl.BlockSpec((1, mask.shape[1], cols), lambda i, w: (block_of(i, w), 0, 0)),
        pl.BlockSpec((cols, width), lambda i, w: (0, 0)),
    ]
    slices = width // thin
    part = [pl.BlockSpec((block, thin), lambda i, w: (i, 0))] * slices
    if merge is None:
        kernel, extra = away_kernel, ()
        out_shape = [jax.ShapeDtypeStruct((zs * block, thin), jnp.bfloat16)] * slices
        out_specs = part
    else:
        recv, panel, start, kind, pieces = merge
        kernel, extra = functools.partial(here_kernel, slices), (panel, start, *recv)
        full = panel.shape[1]
        term = pl.BlockSpec((full, width), lambda i, w: (0, 0))
        in_specs += [pl.BlockSpec((block, full), lambda i, w: (block_of(i, w), 0)), term] + part
        piece = width // pieces
        out_shape = [jax.ShapeDtypeStruct((zs * block, piece), kind)] * pieces
        out_shape.append(jax.ShapeDtypeStruct((full, width), jnp.float32))
        out_specs = [pl.BlockSpec((block, piece), lambda i, w: (i, 0))] * pieces + [term]
    return pl.pallas_call(
        kernel,
        out_shape=out_shape,
        grid_spec=pltpu.PrefetchScalarGridSpec(
            num_scalar_prefetch=1, grid=(zs,), in_specs=in_specs, out_specs=out_specs
        ),
        compiler_params=pltpu.CompilerParams(vmem_limit_bytes=40 * 2**20),
        cost_estimate=pl.CostEstimate(
            flops=2 * zs * block * cols, bytes_accessed=zs * block * width, transcendentals=0
        ),
    )(place, weight, inverse, mask, factor, *extra)


def fetch_factor(panel, cols, columns, detour, row, col, *deps):
    n_row, n_col = lax.axis_size("row"), lax.axis_size("col")
    zs, ratio = n_col // CORES, n_col // n_row
    first, width = columns

    def mirror(j):
        return (zs - 1 - j // CORES) * CORES + j % CORES

    def cross(x, place):
        got = None
        for d in range(1, n_row):
            pairs = []
            for j in range(n_col):
                owner = j // ratio
                pairs.append((owner * n_col + place(j), (owner + d) % n_row * n_col + place(j)))
            arrived = lax.ppermute(x, ("row", "col"), pairs)
            got = arrived if got is None else got + arrived
        return x if got is None else got

    far = cols // 4 if detour and n_row == 2 and zs > 1 else 0
    own = lax.dynamic_slice(panel, (col % ratio * cols, first), (cols, width))
    got = [cross(after(own[:cols - far], *deps), lambda j: j)]
    if far > 0:
        other = lax.dynamic_slice(panel, (mirror(col) % ratio * cols + cols - far, first), (far, width))
        crossed = cross(after(other, *deps), mirror)
        got.append(lax.ppermute(crossed, "col", [(j, mirror(j)) for j in range(n_col)]))
    return own, got


def body(inv_block, block_masks, panel_first, panel_second, diag_inverse, weights):
    n_row, n_col, n_pole = (lax.axis_size(a) for a in ("row", "col", "pole"))
    row, col, pole = (lax.axis_index(a) for a in ("row", "col", "pole"))
    zs = n_col // CORES
    z, core = col // CORES, col % CORES
    inverse, weight = inv_block[0], weights[0]
    rows, cols = inverse.shape
    width = panel_first.shape[2]
    blocks = n_col * n_pole
    block = rows // blocks
    sizes = (zs, block, n_pole, width // SLICES)
    panels = (panel_first[0], panel_second[0])
    grain = rows // block_masks.shape[1]
    groups = max(1, block // grain)

    ratio = n_col // n_row
    mine = row == col // ratio
    half = width // 2
    own, got = [], []
    for k, first, size, _ in PARTS:
        columns = (first * half, size * half)
        mine_rows, others = fetch_factor(panels[k], cols, columns, k == 0, row, col, *(got[-1] if got else ()))
        own.append(mine_rows)
        got.append(others)

    masks = []
    for k in range(2):
        mask = jnp.repeat(block_masks[k].astype(jnp.bfloat16), grain * groups // block, axis=0)
        masks.append(jnp.repeat(mask, grain, axis=1).reshape(blocks, groups, cols))

    def place(c, d, *deps):
        return after(jnp.stack([c, (pole + d) % n_pole]).astype(jnp.int32), *deps)

    dests = list(range(1, n_pole)) + [0]
    token = tuple(masks)
    units, terms = [], [[], []]
    for part, (k, first, size, pieces) in enumerate(PARTS):
        wide = size * half
        factor, start = [], 0
        for x in got[part]:
            x = after(x, *token)
            factor.append(jnp.where(mine, own[part][start:start + x.shape[0]], x))
            start += x.shape[0]
        factor = jnp.concatenate(factor)
        received, arrived = {}, [[] for _ in range(pieces)]
        for d in dests:
            if d == 0:
                token += tuple(unit.step() for unit in units[:-1] if not unit.done())
            away = product(inverse, masks[k], factor, place(1 - core, d, *token), weights, sizes)
            token = (away[0],)
            received[d] = [swap_core(x) for x in away]
        term = jnp.zeros((width, wide), jnp.float32)
        for d in dests:
            if d == 0:
                done = [unit for unit in units if unit.done()]
                token += tuple(unit.step() for unit in units if not unit.done())
            kind = jnp.bfloat16 if d > 0 else jnp.float32
            merge = (received[d], panels[k], term, kind, pieces)
            spot = place(core, d, *token)
            if d == 0:
                for unit in done:
                    spot, unit.total = lax.optimization_barrier((spot, unit.result()))
            *out, term = product(inverse, masks[k], factor, spot, weights, sizes, merge)
            token = (out[0],)
            if d > 0:
                before = ()
                for n, x in enumerate(out):
                    came = lax.ppermute(after(x, *before), "pole", [(i, (i + d) % n_pole) for i in range(n_pole)])
                    before = (came,)
                    arrived[n].append(came)
        terms[k].append(term)
        for n, kept in enumerate(out):
            units.append(ZSum([x.reshape(zs, block, x.shape[1]) for x in [kept] + arrived[n]], z))

    *zeros, early, last = units
    split = (2, n_row, CORES, width // (n_row * CORES), width)
    term = jnp.stack([jnp.concatenate(t, axis=1) for t in terms]).reshape(split)
    term = halve(term, 2, core, swap_core, jnp.float32)
    term = after(term, early.step(*token))
    for unit in zeros:
        while not unit.done():
            term = after(term, unit.step())
    term = halve(term, 1, row, swap_row, jnp.bfloat16)
    term, *firsts = lax.optimization_barrier((term, *[unit.result() for unit in zeros]))
    first = jnp.concatenate(firsts, axis=1)
    squares = jnp.sum(first * first, axis=0)
    bits = zs.bit_length() - 1
    for bit in range(bits):
        if bit == 0:
            term = after(term, last.step(term))
        term, squares = add_both(term, squares, swap_z, 1 << bit)
    while not early.done():
        term = after(term, early.step(term))
    base = pick(pick(diag_inverse.reshape(split), core, 2), row, 1).astype(jnp.float32) * weight
    term = jnp.stack([base[0] + term[0], base[1], term[1]])
    for bit in range(n_pole.bit_length() - 1):
        term, squares = add_both(term, squares, swap_pole, 1 << bit, exact=True)
    while not last.done():
        term = after(term, last.step(term))
    piece = term.astype(jnp.bfloat16)[:, None, None]
    for bit in reversed(range(n_row.bit_length() - 1)):
        piece, squares = double(piece, squares, 1, row, bit, swap_row)
    piece, second = lax.optimization_barrier((piece, early.result(piece)))
    piece, squares = double(piece, squares, 2, core, 0, swap_core)
    second = [second, last.result()]
    scale = jnp.sqrt(squares / (rows * n_row) + 1e-06)
    piece = piece.reshape(3, width, width).astype(jnp.float32)
    scaled = piece[1] + piece[2] / (scale[:, None] * scale)
    second = jnp.concatenate(second, axis=1) / scale
    return jnp.stack([first.astype(jnp.bfloat16), second.astype(jnp.bfloat16)]), jnp.stack([piece[0], scaled])


def solution(mesh):
    placed = (
        P("pole", "row", "col"),
        P(None, "row", "col"),
        P("pole", "row", None),
        P("pole", "row", None),
        P(None, "pole", None, None),
        P("pole"),
    )
    return jax.shard_map(
        body,
        mesh=mesh,
        in_specs=placed,
        out_specs=(P(None, ("row", "col", "pole"), None), P()),
        check_vma=False,
    )
```

```python
import functools

import jax
import jax.numpy as jnp
from jax import lax
from jax.experimental import pallas as pl
from jax.experimental.pallas import tpu as pltpu
from jax.sharding import PartitionSpec as P

CORES = 2
SLICES = 4
PARTS = ((0, 0, 2, 1), (1, 0, 2, 2))


def swap(x, axis, mask):
    size = lax.axis_size(axis)
    return lax.ppermute(x, axis, [(i, i ^ mask) for i in range(size)])


def swap_core(x, mask=1):
    return swap(x, "col", mask)


def swap_z(x, mask):
    return swap(x, "col", mask * CORES)


def swap_row(x, mask):
    return swap(x, "row", mask)


def swap_pole(x, mask):
    return swap(x, "pole", mask)


def after(x, *deps):
    if not deps:
        return x
    return lax.optimization_barrier((x,) + deps)[0]


def pick(x, index, axis):
    return lax.dynamic_index_in_dim(x, index, axis, keepdims=False)


def halve(x, axis, index, exchange, kind, before_last=None):
    bit = 0
    while x.shape[axis] > 1:
        size = x.shape[axis]
        if size == 2 and before_last is not None:
            x = before_last(x)
        pairs = x.reshape(x.shape[:axis] + (size // 2, 2) + x.shape[axis + 1:])
        low = (index >> bit) & 1
        send = pick(pairs, 1 - low, axis + 1).astype(kind)
        x = pick(pairs, low, axis + 1).astype(jnp.float32) + exchange(send, 1 << bit).astype(jnp.float32)
        bit += 1
    return x.reshape(x.shape[:axis] + x.shape[axis + 1:])


def split_three(x):
    terms = []
    for _ in range(3):
        high = lax.reduce_precision(x, 8, 7)
        terms.append(high.astype(jnp.bfloat16))
        x = x - high
    return jnp.stack(terms)


def double(x, squares, axis, index, bit, exchange):
    count = x.size // x.shape[-1]
    message = jnp.concatenate([x.reshape(count, x.shape[-1]), split_three(squares)])
    other = exchange(message, 1 << bit)
    squares = squares + jnp.sum(other[count:].astype(jnp.float32), axis=0)
    other = other[:count].reshape(x.shape)
    low = (index >> bit) & 1
    both = jnp.where(low == 0, jnp.stack([x, other], axis + 1), jnp.stack([other, x], axis + 1))
    return both.reshape(x.shape[:axis] + (2 * x.shape[axis],) + x.shape[axis + 1:]), squares


class ZSum:
    def __init__(self, sources, z):
        self.sources, self.z, self.bit = [(x, 0) for x in sources], z, 0
        self.bits = sources[0].shape[0].bit_length() - 1
        self.total = None

    def part(self, flip, *deps):
        total = 0.0
        for x, depth in self.sources:
            spread = 1 << (self.bit - depth + flip)
            index = (self.z >> depth) & (spread - 1)
            if flip:
                index = index ^ (spread >> 1)
            x = x.reshape((x.shape[0] // spread, spread) + x.shape[1:])
            total = total + pick(after(x, *deps), index, 1).astype(jnp.float32)
        return total

    def step(self, *deps):
        send = self.part(1, *deps).astype(jnp.bfloat16)
        came = swap_z(send, 1 << self.bit)
        self.bit += 1
        self.sources.append((came, self.bit))
        return send

    def done(self):
        return self.bit == self.bits

    def result(self, *deps):
        if self.total is not None:
            return self.total
        x = self.part(0, *deps)
        return x.reshape(x.shape[1:])


def weighted_product(a_ref, mask_ref, f_ref, weight_ref):
    rows, cols = a_ref.shape
    groups = mask_ref.shape[1]
    shaped = a_ref[...].reshape(groups, rows // groups, cols)
    masked = (shaped * mask_ref[0][:, None, :]).reshape(rows, cols)
    return jnp.dot(masked, f_ref[...], preferred_element_type=jnp.float32) * weight_ref[0]


def away_kernel(where_ref, weight_ref, a_ref, mask_ref, f_ref, *outs):
    total = weighted_product(a_ref, mask_ref, f_ref, weight_ref)
    width = total.shape[1] // len(outs)
    for n, out_ref in enumerate(outs):
        out_ref[...] = total[:, n * width:(n + 1) * width].astype(out_ref.dtype)


def here_kernel(slices, where_ref, weight_ref, a_ref, mask_ref, f_ref, panel_ref, start_ref, *refs):
    recvs, outs, term_ref = refs[:slices], refs[slices:-1], refs[-1]
    total = weighted_product(a_ref, mask_ref, f_ref, weight_ref)
    total = total + jnp.concatenate([r[...].astype(jnp.float32) for r in recvs], axis=1)
    width = total.shape[1] // len(outs)
    for n, out_ref in enumerate(outs):
        out_ref[...] = total[:, n * width:(n + 1) * width].astype(out_ref.dtype)
    term = lax.dot_general(
        panel_ref[...], total.astype(jnp.bfloat16), (((0,), (0,)), ((), ())), preferred_element_type=jnp.float32
    )

    @pl.when(pl.program_id(0) == 0)
    def _():
        term_ref[...] = start_ref[...] - term

    @pl.when(pl.program_id(0) > 0)
    def _():
        term_ref[...] = term_ref[...] - term


def product(inverse, mask, factor, place, weight, sizes, merge=None):
    zs, block, n_pole, thin = sizes
    cols = inverse.shape[1]
    width = factor.shape[1]

    def block_of(i, where):
        return (i * CORES + where[0]) * n_pole + where[1]

    in_specs = [
        pl.BlockSpec(memory_space=pltpu.SMEM),
        pl.BlockSpec((block, cols), lambda i, w: (block_of(i, w), 0)),
        pl.BlockSpec((1, mask.shape[1], cols), lambda i, w: (block_of(i, w), 0, 0)),
        pl.BlockSpec((cols, width), lambda i, w: (0, 0)),
    ]
    slices = width // thin
    part = [pl.BlockSpec((block, thin), lambda i, w: (i, 0))] * slices
    if merge is None:
        kernel, extra = away_kernel, ()
        out_shape = [jax.ShapeDtypeStruct((zs * block, thin), jnp.bfloat16)] * slices
        out_specs = part
    else:
        recv, panel, start, kind, pieces = merge
        kernel, extra = functools.partial(here_kernel, slices), (panel, start, *recv)
        full = panel.shape[1]
        term = pl.BlockSpec((full, width), lambda i, w: (0, 0))
        in_specs += [pl.BlockSpec((block, full), lambda i, w: (block_of(i, w), 0)), term] + part
        piece = width // pieces
        out_shape = [jax.ShapeDtypeStruct((zs * block, piece), kind)] * pieces
        out_shape.append(jax.ShapeDtypeStruct((full, width), jnp.float32))
        out_specs = [pl.BlockSpec((block, piece), lambda i, w: (i, 0))] * pieces + [term]
    return pl.pallas_call(
        kernel,
        out_shape=out_shape,
        grid_spec=pltpu.PrefetchScalarGridSpec(
            num_scalar_prefetch=1, grid=(zs,), in_specs=in_specs, out_specs=out_specs
        ),
        compiler_params=pltpu.CompilerParams(vmem_limit_bytes=40 * 2**20),
        cost_estimate=pl.CostEstimate(
            flops=2 * zs * block * cols, bytes_accessed=zs * block * width, transcendentals=0
        ),
    )(place, weight, inverse, mask, factor, *extra)


def fetch_factor(panel, cols, columns, detour, row, col, *deps):
    n_row, n_col = lax.axis_size("row"), lax.axis_size("col")
    zs, ratio = n_col // CORES, n_col // n_row
    first, width = columns

    def mirror(j):
        return (zs - 1 - j // CORES) * CORES + j % CORES

    def cross(x, place):
        got = None
        for d in range(1, n_row):
            pairs = []
            for j in range(n_col):
                owner = j // ratio
                pairs.append((owner * n_col + place(j), (owner + d) % n_row * n_col + place(j)))
            arrived = lax.ppermute(x, ("row", "col"), pairs)
            got = arrived if got is None else got + arrived
        return x if got is None else got

    far = cols // 4 if detour and n_row == 2 and zs > 1 else 0
    own = lax.dynamic_slice(panel, (col % ratio * cols, first), (cols, width))
    got = [cross(after(own[:cols - far], *deps), lambda j: j)]
    if far > 0:
        other = lax.dynamic_slice(panel, (mirror(col) % ratio * cols + cols - far, first), (far, width))
        crossed = cross(after(other, *deps), mirror)
        got.append(lax.ppermute(crossed, "col", [(j, mirror(j)) for j in range(n_col)]))
    return own, got


def body(inv_block, block_masks, panel_first, panel_second, diag_inverse, weights):
    n_row, n_col, n_pole = (lax.axis_size(a) for a in ("row", "col", "pole"))
    row, col, pole = (lax.axis_index(a) for a in ("row", "col", "pole"))
    zs = n_col // CORES
    z, core = col // CORES, col % CORES
    inverse, weight = inv_block[0], weights[0]
    rows, cols = inverse.shape
    width = panel_first.shape[2]
    blocks = n_col * n_pole
    block = rows // blocks
    sizes = (zs, block, n_pole, width // SLICES)
    panels = (panel_first[0], panel_second[0])
    grain = rows // block_masks.shape[1]
    groups = max(1, block // grain)

    ratio = n_col // n_row
    mine = row == col // ratio
    half = width // 2
    own, got = [], []
    for k, first, size, _ in PARTS:
        columns = (first * half, size * half)
        mine_rows, others = fetch_factor(panels[k], cols, columns, k == 0, row, col, *(got[-1] if got else ()))
        own.append(mine_rows)
        got.append(others)

    masks = []
    for k in range(2):
        mask = jnp.repeat(block_masks[k].astype(jnp.bfloat16), grain * groups // block, axis=0)
        masks.append(jnp.repeat(mask, grain, axis=1).reshape(blocks, groups, cols))

    def place(c, d, *deps):
        return after(jnp.stack([c, (pole + d) % n_pole]).astype(jnp.int32), *deps)

    dests = list(range(1, n_pole)) + [0]
    token = tuple(masks)
    units, terms = [], [[], []]
    for part, (k, first, size, pieces) in enumerate(PARTS):
        wide = size * half
        factor, start = [], 0
        for x in got[part]:
            x = after(x, *token)
            factor.append(jnp.where(mine, own[part][start:start + x.shape[0]], x))
            start += x.shape[0]
        factor = jnp.concatenate(factor)
        arrived = [[] for _ in range(pieces)]
        term = jnp.zeros((width, wide), jnp.float32)
        for d in dests:
            if d == 0:
                token += tuple(unit.step() for unit in units if not unit.done())
            away = product(inverse, masks[k], factor, place(1 - core, d, *token), weights, sizes)
            token = (away[0],)
            received = [swap_core(x) for x in away]
            kind = jnp.bfloat16 if d > 0 else jnp.float32
            merge = (received, panels[k], term, kind, pieces)
            *out, term = product(inverse, masks[k], factor, place(core, d, *token), weights, sizes, merge)
            token = (out[0],)
            if d > 0:
                before = ()
                for n, x in enumerate(out):
                    came = lax.ppermute(after(x, *before), "pole", [(i, (i + d) % n_pole) for i in range(n_pole)])
                    before = (came,)
                    arrived[n].append(came)
        terms[k].append(term)
        for n, kept in enumerate(out):
            units.append(ZSum([x.reshape(zs, block, x.shape[1]) for x in [kept] + arrived[n]], z))

    *zeros, early, last = units

    def arrivals(x):
        x = after(x, last.step())
        while not early.done():
            x = after(x, early.step())
        for unit in zeros:
            x, unit.total = lax.optimization_barrier((x, unit.result()))
        return x

    each = width // (n_row * blocks)
    split = (2, n_row, zs, CORES, n_pole, each, width)
    term = jnp.stack([jnp.concatenate(t, axis=1) for t in terms]).reshape(split)
    term = after(term, early.step(*token))
    for unit in zeros:
        while not unit.done():
            term = after(term, unit.step())
    term = halve(term, 3, core, swap_core, jnp.bfloat16)
    term = halve(term, 1, row, swap_row, jnp.bfloat16)
    term = halve(term, 1, z, swap_z, jnp.bfloat16, arrivals)
    base = pick(pick(pick(diag_inverse.reshape(split), core, 3), row, 1), z, 1).astype(jnp.float32) * weight
    both = halve(jnp.stack([base, term]), 2, pole, swap_pole, jnp.float32)
    base, term = both[0], both[1]
    piece = jnp.stack([base[0] + term[0], base[1], term[1]]).astype(jnp.bfloat16)
    piece = piece[:, None, None, None, None]
    piece, *firsts = lax.optimization_barrier((piece, *[unit.result() for unit in zeros]))
    first = jnp.concatenate(firsts, axis=1)
    squares = jnp.sum(first * first, axis=0)
    for bit in reversed(range(n_pole.bit_length() - 1)):
        piece, squares = double(piece, squares, 4, pole, bit, swap_pole)
    piece, second = lax.optimization_barrier((piece, early.result(piece)))
    for bit in reversed(range(zs.bit_length() - 1)):
        if not last.done():
            piece = after(piece, last.step(piece))
        piece, squares = double(piece, squares, 2, z, bit, swap_z)
    for bit in reversed(range(n_row.bit_length() - 1)):
        piece, squares = double(piece, squares, 1, row, bit, swap_row)
    while not last.done():
        piece = after(piece, last.step(piece))
    piece, *second = lax.optimization_barrier((piece, second, last.result(piece)))
    piece, squares = double(piece, squares, 3, core, 0, swap_core)
    scale = jnp.sqrt(squares / (rows * n_row) + 1e-06)
    piece = piece.reshape(3, width, width).astype(jnp.float32)
    scaled = piece[1] + piece[2] / (scale[:, None] * scale)
    second = jnp.concatenate(second, axis=1) / scale
    return jnp.stack([first.astype(jnp.bfloat16), second.astype(jnp.bfloat16)]), jnp.stack([piece[0], scaled])


def solution(mesh):
    placed = (
        P("pole", "row", "col"),
        P(None, "row", "col"),
        P("pole", "row", None),
        P("pole", "row", None),
        P(None, "pole", None, None),
        P("pole"),
    )
    return jax.shard_map(
        body,
        mesh=mesh,
        in_specs=placed,
        out_specs=(P(None, ("row", "col", "pole"), None), P()),
        check_vma=False,
    )
```

```python
import jax
import jax.numpy as jnp
from jax import lax
from jax.experimental import pallas as pl
from jax.experimental.pallas import tpu as pltpu
from jax.sharding import PartitionSpec as P

CORES = 2
AWAY = 2
PIECES = (1, 2)


def swap(x, axis, mask):
    size = lax.axis_size(axis)
    return lax.ppermute(x, axis, [(i, i ^ mask) for i in range(size)])


def swap_core(x, mask=1):
    return swap(x, "col", mask)


def swap_z(x, mask):
    return swap(x, "col", mask * CORES)


def swap_row(x, mask):
    return swap(x, "row", mask)


def swap_pole(x, mask):
    return swap(x, "pole", mask)


def after(x, *deps):
    if not deps:
        return x
    return lax.optimization_barrier((x,) + deps)[0]


def pick(x, index, axis):
    return lax.dynamic_index_in_dim(x, index, axis, keepdims=False)


def halve(x, axis, index, exchange, kind):
    bit = 0
    while x.shape[axis] > 1:
        size = x.shape[axis]
        pairs = x.reshape(x.shape[:axis] + (size // 2, 2) + x.shape[axis + 1:])
        low = (index >> bit) & 1
        send = pick(pairs, 1 - low, axis + 1).astype(kind)
        x = pick(pairs, low, axis + 1).astype(jnp.float32) + exchange(send, 1 << bit).astype(jnp.float32)
        bit += 1
    return x.reshape(x.shape[:axis] + x.shape[axis + 1:])


def split_three(x):
    terms = []
    for _ in range(3):
        high = lax.reduce_precision(x, 8, 7)
        terms.append(high.astype(jnp.bfloat16))
        x = x - high
    return jnp.stack(terms)


def double(x, squares, axis, index, bit, exchange):
    count = x.size // x.shape[-1]
    message = jnp.concatenate([x.reshape(count, x.shape[-1]), split_three(squares)])
    other = exchange(message, 1 << bit)
    squares = squares + jnp.sum(other[count:].astype(jnp.float32), axis=0)
    other = other[:count].reshape(x.shape)
    low = (index >> bit) & 1
    both = jnp.where(low == 0, jnp.stack([x, other], axis + 1), jnp.stack([other, x], axis + 1))
    return both.reshape(x.shape[:axis] + (2 * x.shape[axis],) + x.shape[axis + 1:]), squares


class ZSum:
    def __init__(self, sources, z):
        self.sources, self.z, self.bit = [(x, 0) for x in sources], z, 0
        self.bits = sources[0].shape[0].bit_length() - 1

    def part(self, flip, *deps):
        total = 0.0
        for x, depth in self.sources:
            spread = 1 << (self.bit - depth + flip)
            index = (self.z >> depth) & (spread - 1)
            if flip:
                index = index ^ (spread >> 1)
            x = x.reshape((x.shape[0] // spread, spread) + x.shape[1:])
            total = total + pick(after(x, *deps), index, 1).astype(jnp.float32)
        return total

    def step(self, *deps):
        send = self.part(1, *deps).astype(jnp.bfloat16)
        came = swap_z(send, 1 << self.bit)
        self.bit += 1
        self.sources.append((came, self.bit))
        return send

    def done(self):
        return self.bit == self.bits

    def result(self, *deps):
        x = self.part(0, *deps)
        return x.reshape(x.shape[1:])


def weighted_product(a_ref, mask_ref, f_ref, weight_ref):
    rows, cols = a_ref.shape
    groups = mask_ref.shape[1]
    shaped = a_ref[...].reshape(groups, rows // groups, cols)
    masked = (shaped * mask_ref[0][:, None, :]).reshape(rows, cols)
    return jnp.dot(masked, f_ref[...], preferred_element_type=jnp.float32) * weight_ref[0]


def away_kernel(where_ref, weight_ref, a_ref, mask_ref, f_ref, *outs):
    total = weighted_product(a_ref, mask_ref, f_ref, weight_ref)
    width = total.shape[1] // len(outs)
    for n, out_ref in enumerate(outs):
        out_ref[...] = total[:, n * width:(n + 1) * width].astype(out_ref.dtype)


def here_kernel(where_ref, weight_ref, a_ref, mask_ref, f_ref, panel_ref, start_ref, *refs):
    recvs, outs, term_ref = refs[:AWAY], refs[AWAY:-1], refs[-1]
    total = weighted_product(a_ref, mask_ref, f_ref, weight_ref)
    total = total + jnp.concatenate([r[...].astype(jnp.float32) for r in recvs], axis=1)
    width = total.shape[1] // len(outs)
    for n, out_ref in enumerate(outs):
        out_ref[...] = total[:, n * width:(n + 1) * width].astype(out_ref.dtype)
    term = lax.dot_general(
        panel_ref[...], total.astype(jnp.bfloat16), (((0,), (0,)), ((), ())), preferred_element_type=jnp.float32
    )

    @pl.when(pl.program_id(0) == 0)
    def _():
        term_ref[...] = start_ref[...] - term

    @pl.when(pl.program_id(0) > 0)
    def _():
        term_ref[...] = term_ref[...] - term


def product(inverse, mask, factor, place, weight, sizes, merge=None):
    zs, block, n_pole = sizes
    cols = inverse.shape[1]
    width = factor.shape[1]

    def block_of(i, where):
        return (i * CORES + where[0]) * n_pole + where[1]

    in_specs = [
        pl.BlockSpec(memory_space=pltpu.SMEM),
        pl.BlockSpec((block, cols), lambda i, w: (block_of(i, w), 0)),
        pl.BlockSpec((1, mask.shape[1], cols), lambda i, w: (block_of(i, w), 0, 0)),
        pl.BlockSpec((cols, width), lambda i, w: (0, 0)),
    ]
    part = [pl.BlockSpec((block, width // AWAY), lambda i, w: (i, 0))] * AWAY
    if merge is None:
        kernel, extra = away_kernel, ()
        out_shape = [jax.ShapeDtypeStruct((zs * block, width // AWAY), jnp.bfloat16)] * AWAY
        out_specs = part
    else:
        recv, panel, start, kind, pieces = merge
        kernel, extra = here_kernel, (panel, start, *recv)
        full = panel.shape[1]
        term = pl.BlockSpec((full, width), lambda i, w: (0, 0))
        in_specs += [pl.BlockSpec((block, full), lambda i, w: (block_of(i, w), 0)), term] + part
        piece = width // pieces
        out_shape = [jax.ShapeDtypeStruct((zs * block, piece), kind)] * pieces
        out_shape.append(jax.ShapeDtypeStruct((full, width), jnp.float32))
        out_specs = [pl.BlockSpec((block, piece), lambda i, w: (i, 0))] * pieces + [term]
    return pl.pallas_call(
        kernel,
        out_shape=out_shape,
        grid_spec=pltpu.PrefetchScalarGridSpec(
            num_scalar_prefetch=1, grid=(zs,), in_specs=in_specs, out_specs=out_specs
        ),
        compiler_params=pltpu.CompilerParams(vmem_limit_bytes=40 * 2**20),
        cost_estimate=pl.CostEstimate(
            flops=2 * zs * block * cols, bytes_accessed=zs * block * width, transcendentals=0
        ),
    )(place, weight, inverse, mask, factor, *extra)


def fetch_factor(own):
    n_row, n_col = lax.axis_size("row"), lax.axis_size("col")
    if n_row == 2:
        return swap_row(own, 1)
    ratio = n_col // n_row
    got = own
    for d in range(1, n_row):
        pairs = [((j // ratio) * n_col + j, ((j // ratio + d) % n_row) * n_col + j) for j in range(n_col)]
        arrived = lax.ppermute(own, ("row", "col"), pairs)
        got = arrived if d == 1 else got + arrived
    return got


def body(inv_block, block_masks, panel_first, panel_second, diag_inverse, weights):
    n_row, n_col, n_pole = (lax.axis_size(a) for a in ("row", "col", "pole"))
    row, col, pole = (lax.axis_index(a) for a in ("row", "col", "pole"))
    zs = n_col // CORES
    z, core = col // CORES, col % CORES
    inverse, weight = inv_block[0], weights[0]
    rows, cols = inverse.shape
    width = panel_first.shape[2]
    blocks = n_col * n_pole
    block = rows // blocks
    sizes = (zs, block, n_pole)
    panels = (panel_first[0], panel_second[0])
    grain = rows // block_masks.shape[1]
    groups = max(1, block // grain)

    ratio = n_col // n_row
    mine = row == col // ratio
    own, got = [], []
    for panel in panels:
        piece = lax.dynamic_slice(panel, (col % ratio * cols, 0), (cols, width))
        own.append(piece)
        got.append(fetch_factor(after(piece, *got)))

    masks = []
    for k in range(2):
        mask = jnp.repeat(block_masks[k].astype(jnp.bfloat16), grain * groups // block, axis=0)
        masks.append(jnp.repeat(mask, grain, axis=1).reshape(blocks, groups, cols))

    def place(c, d, *deps):
        return after(jnp.stack([c, (pole + d) % n_pole]).astype(jnp.int32), *deps)

    dests = list(range(1, n_pole)) + [0]
    token = tuple(masks)
    units, terms = [], []
    for k in range(2):
        factor = jnp.where(mine, own[k], after(got[k], *token))
        received, arrived = {}, [[] for _ in range(PIECES[k])]
        for d in dests:
            away = product(inverse, masks[k], factor, place(1 - core, d, *token), weights, sizes)
            token = (away[0],)
            received[d] = [swap_core(x) for x in away]
        term = jnp.zeros((width, width), jnp.float32)
        for d in dests:
            if d == 0:
                token += tuple(unit.step() for unit in units)
            kind = jnp.bfloat16 if d > 0 else jnp.float32
            merge = (received[d], panels[k], term, kind, PIECES[k])
            *out, term = product(inverse, masks[k], factor, place(core, d, *token), weights, sizes, merge)
            token = (out[0],)
            if d > 0:
                before = ()
                for n, x in enumerate(out):
                    came = lax.ppermute(after(x, *before), "pole", [(i, (i + d) % n_pole) for i in range(n_pole)])
                    before = (came,)
                    arrived[n].append(came)
        terms.append(term)
        for n, kept in enumerate(out):
            units.append(ZSum([x.reshape(zs, block, x.shape[1]) for x in [kept] + arrived[n]], z))

    zero, early, last = units
    each = width // (n_row * blocks)
    split = (2, n_row, zs, CORES, n_pole, each, width)
    term = halve(jnp.stack(terms).reshape(split), 3, core, swap_core, jnp.bfloat16)
    term = after(term, early.step(*token))
    term = halve(term, 1, row, swap_row, jnp.bfloat16)
    while not zero.done():
        term = after(term, zero.step())
    term = halve(term, 1, z, swap_z, jnp.bfloat16)
    while not early.done():
        term = after(term, early.step(term))
    first = zero.result(term)
    squares = jnp.sum(first * first, axis=0)
    term = after(term, squares, last.step(term))
    base = pick(pick(pick(diag_inverse.reshape(split), core, 3), row, 1), z, 1).astype(jnp.float32) * weight
    both = halve(jnp.stack([base, term]), 2, pole, swap_pole, jnp.float32)
    base, term = both[0], both[1]
    piece = jnp.stack([base[0] + term[0], base[1], term[1]]).astype(jnp.bfloat16)
    piece = piece[:, None, None, None, None]
    for bit in reversed(range(n_pole.bit_length() - 1)):
        piece, squares = double(piece, squares, 4, pole, bit, swap_pole)
    while not last.done():
        piece = after(piece, last.step(piece))
    piece, second = lax.optimization_barrier((piece, early.result(piece)))
    for bit in reversed(range(zs.bit_length() - 1)):
        piece, squares = double(piece, squares, 2, z, bit, swap_z)
    piece, *second = lax.optimization_barrier((piece, second, last.result(piece)))
    for bit in reversed(range(n_row.bit_length() - 1)):
        piece, squares = double(piece, squares, 1, row, bit, swap_row)
    piece, squares = double(piece, squares, 3, core, 0, swap_core)
    scale = jnp.sqrt(squares / (rows * n_row) + 1e-06)
    piece = piece.reshape(3, width, width).astype(jnp.float32)
    scaled = piece[1] + piece[2] / (scale[:, None] * scale)
    second = jnp.concatenate(second, axis=1) / scale
    return jnp.stack([first.astype(jnp.bfloat16), second.astype(jnp.bfloat16)]), jnp.stack([piece[0], scaled])


def solution(mesh):
    placed = (
        P("pole", "row", "col"),
        P(None, "row", "col"),
        P("pole", "row", None),
        P("pole", "row", None),
        P(None, "pole", None, None),
        P("pole"),
    )
    return jax.shard_map(
        body,
        mesh=mesh,
        in_specs=placed,
        out_specs=(P(None, ("row", "col", "pole"), None), P()),
        check_vma=False,
    )
```
